128 devices in a mesh: ifg: 4 (over y_lo, core), rows: 32 (over x, z, y_hi).
Axes of the slice: x: 4, y: 4 (y_hi: 2, y_lo: 2; y = y_hi * 2 + y_lo), z: 4, core: 2. Of those that a mesh axis runs over, the one named last changes fastest.
Arguments:
- phase_samples: bfloat16 [300, 64, 32768], P('ifg', 'rows'), may hold values from -6 to 6
- sample_weights: bfloat16 [300, 64, 32768], P('ifg', 'rows'), may hold values from 0.099609375 to 10
- reference_date: int32 [300], replicated, may hold values from 0 to 158, as said below
- secondary_date: int32 [300], replicated, may hold values from 1 to 159, as said below
- window_rows: int32 [9], replicated, may hold values from -1 to 1, as said below
- window_cols: int32 [9], replicated, may hold values from -4 to 4, as said below
Outputs:
- coherence: float32 [300, 32, 4096], P('ifg', 'rows')
- residual: float32 [300, 32, 4096], P('ifg', 'rows')
- displacement: float32 [159, 32, 4096], P(None, None, ('ifg', 'rows'))
The draws below stay inside these ranges and needn't reach their ends.
Inputs may be any that keep to these rules, and one draw needn't show every extreme that they name: reference_date[k] < secondary_date[k] and secondary_date[k] - reference_date[k] <= 24 for every k; for every date d < 159 some interferogram has reference d and secondary d + 1. `secondary_date`: pairs with reference_date as stated there. `window_rows`: entry 0 is 0 and both -1 and 1 occur. `window_cols`: entry 0 is 0 and both -4 and 4 occur.
All inputs are finite; a program needn't handle non-finite values.
Results may differ from the reference program's by a relative error of at most 0.0003.
Values sent between devices are 32-bit elements; how exact they have to be, the bound alone decides.
No kernel may reach another device: no remote copies, remote signals or barrier semaphores. Data moves between devices by JAX's collectives and lax.ppermute only.
A program may use at most 192 MiB of HBM per device.

```python
import math
import jax
import jax.numpy as jnp
from jax import lax

IFGS = 300
DATES = 160
AZ_LOOKS = 2
RG_LOOKS = 8
HALF_WIN = 1
COL_REACH = 4
OFFSETS = 9
FULL_ROWS = 64
FULL_COLS = 32768


def network_pairs(key):
    base_key = jax.random.fold_in(key, 7)
    start_key, span_key, order_key = jax.random.split(base_key, 3)
    extra_count = IFGS - (DATES - 1)
    chain = jnp.arange(DATES - 1, dtype=jnp.int32)
    starts = jax.random.randint(start_key, (extra_count,), 0, DATES - 2, dtype=jnp.int32)
    spans = jax.random.randint(span_key, (extra_count,), 2, 25, dtype=jnp.int32)
    ends = jnp.minimum(starts + spans, DATES - 1)
    firsts = jnp.concatenate([chain, starts])
    seconds = jnp.concatenate([chain + 1, ends])
    order = jax.random.permutation(order_key, IFGS)
    return (firsts[order].astype(jnp.int32), seconds[order].astype(jnp.int32))


def draw_reference_date(key, part):
    return network_pairs(key)[0]


def draw_secondary_date(key, part):
    return network_pairs(key)[1]


def draw_window_rows(key, part):
    row_key = jax.random.fold_in(key, 11)
    values = jax.random.randint(row_key, (OFFSETS,), -HALF_WIN, HALF_WIN + 1, dtype=jnp.int32)
    return values.at[0].set(0).at[1].set(-HALF_WIN).at[2].set(HALF_WIN)


def draw_window_cols(key, part):
    col_key = jax.random.fold_in(key, 13)
    values = jax.random.randint(col_key, (OFFSETS,), -COL_REACH, COL_REACH + 1, dtype=jnp.int32)
    return values.at[0].set(0).at[3].set(-COL_REACH).at[4].set(COL_REACH)


def steps_of(rng, shape, cuts, smallest, largest):
    level = 1.0
    for axis_at, shards_of in cuts:
        heights = jax.random.uniform(jax.random.fold_in(jax.random.fold_in(rng, 6), axis_at), (shards_of,), jnp.float32, smallest / len(cuts), largest / len(cuts))
        level = level * jnp.repeat(jnp.exp(heights), shape[axis_at] // shards_of).reshape((-1,) + (1,) * (len(shape) - 1 - axis_at))
    return level


def noise(rng, dims, scale, limit, pieces=(), held_as=jnp.bfloat16):
    result = jax.random.normal(rng, dims, jnp.float32) * scale
    if len(pieces) > 0:
        result = steps_of(rng, dims, pieces, -0.22, 0.18) * result
    return jnp.clip(result, min=-limit, max=limit).astype(held_as)


def setup_inputs(seed: int = 0) -> dict:
    arg_keys = jax.random.split(jax.random.key(seed), 7)
    return {
        "phase_samples": noise(arg_keys[0], (IFGS, FULL_ROWS, FULL_COLS), 1.0, 6.0, ((0, 4), (1, 32))),
        "sample_weights": jnp.clip(jnp.exp(math.log(10.0) - 4.609084 * jax.random.uniform(arg_keys[1], (IFGS, FULL_ROWS, FULL_COLS), jnp.float32) ** steps_of(arg_keys[1], (IFGS, FULL_ROWS, FULL_COLS), ((0, 4), (1, 32)), -0.2, 0.2)), 0.099609375, 10.0).astype(jnp.bfloat16),
        "reference_date": draw_reference_date(jax.random.fold_in(arg_keys[6], 71), 0),
        "secondary_date": draw_secondary_date(jax.random.fold_in(arg_keys[6], 71), 0),
        "window_rows": draw_window_rows(jax.random.fold_in(arg_keys[6], 71), 0),
        "window_cols": draw_window_cols(jax.random.fold_in(arg_keys[6], 71), 0),
    }


damping = 0.25

def network_solve(reference_date, secondary_date):
    date_index = jnp.arange(DATES, dtype=jnp.int32)
    signed = (secondary_date[:, None] == date_index[None, :]).astype(jnp.float32) - (reference_date[:, None] == date_index[None, :]).astype(jnp.float32)
    design = signed[:, 1:]
    normal_matrix = jnp.dot(design.T.astype(jnp.float32), design.astype(jnp.float32), precision=lax.Precision.HIGHEST, preferred_element_type=jnp.float32)
    normal_matrix = normal_matrix + damping * jnp.eye(DATES - 1, dtype=jnp.float32)
    factor = jnp.linalg.cholesky(normal_matrix)
    inverse = jax.scipy.linalg.cho_solve((factor, True), design.T)
    return (design, inverse)

def pool_looks(values):
    look_rows = values.shape[0] // AZ_LOOKS
    look_cols = values.shape[1] // RG_LOOKS
    return values.reshape(look_rows, AZ_LOOKS, look_cols, RG_LOOKS).sum(axis=(1, 3))

def reference(phase_samples, sample_weights, reference_date, secondary_date, window_rows, window_cols):
    design, inverse = network_solve(reference_date, secondary_date)

    def one_interferogram(pair):
        phase_float = pair[0].astype(jnp.float32)
        weight_float = pair[1].astype(jnp.float32)
        look_weight = pool_looks(weight_float)
        look_phase = pool_looks(weight_float * phase_float)
        look_cos = pool_looks(weight_float * jnp.cos(phase_float))
        look_sin = pool_looks(weight_float * jnp.sin(phase_float))
        multilooked = look_phase / look_weight
        stacked = jnp.stack([look_cos, look_sin, look_weight])
        padded = jnp.pad(stacked, ((0, 0), (HALF_WIN, HALF_WIN), (COL_REACH, COL_REACH)))
        total = jnp.zeros(stacked.shape, jnp.float32)
        zero_index = jnp.zeros((), jnp.int32)
        for offset_index in range(OFFSETS):
            start_row = (HALF_WIN + window_rows[offset_index]).astype(jnp.int32)
            start_col = (COL_REACH + window_cols[offset_index]).astype(jnp.int32)
            total = total + lax.dynamic_slice(padded, (zero_index, start_row, start_col), stacked.shape)
        coherence = jnp.sqrt(total[0] * total[0] + total[1] * total[1]) / total[2]
        return (multilooked, coherence)
    multilooked, coherence = lax.map(one_interferogram, (phase_samples, sample_weights))
    flat_phase = multilooked.reshape(multilooked.shape[0], -1)
    displacement = jnp.dot(inverse.astype(jnp.float32), flat_phase.astype(jnp.float32), precision=lax.Precision.HIGHEST, preferred_element_type=jnp.float32)
    residual = flat_phase - jnp.dot(design.astype(jnp.float32), displacement.astype(jnp.float32), precision=lax.Precision.HIGHEST, preferred_element_type=jnp.float32)
    return (coherence, residual.reshape(multilooked.shape), displacement.reshape(DATES - 1, multilooked.shape[1], multilooked.shape[2]))
```

```python
import math

import jax
import jax.numpy as jnp
from jax import lax
from jax.experimental import pallas as pl
from jax.experimental.pallas import tpu as pltpu
from jax.sharding import PartitionSpec as P

DATES = 160
AZ_LOOKS = 2
RG_LOOKS = 8
COL_REACH = 4
OFFSETS = 9
LANES = 128

damping = 0.25

SIN_QUARTER = (
    0.3535533845424652,
    -0.0036828448064625263,
    1.1508434909046628e-05,
    -1.7096880355893518e-08,
    1.4046378643550739e-11,
)
COS_QUARTER = (
    0.9999999403953552,
    -0.031249957159161568,
    0.00016275106463581324,
    -3.383578359716921e-07,
    3.553040917037009e-10,
)
SIN_SCALE = 2.0 * math.sqrt(2.0)

PIECES = 16
GROUP = 16


def network_solve(reference_date, secondary_date):
    date_index = jnp.arange(DATES, dtype=jnp.int32)
    signed = (secondary_date[:, None] == date_index[None, :]).astype(jnp.float32) - (
        reference_date[:, None] == date_index[None, :]
    ).astype(jnp.float32)
    design = signed[:, 1:]
    normal_matrix = jnp.dot(
        design.T, design, precision=lax.Precision.HIGHEST, preferred_element_type=jnp.float32
    )
    normal_matrix = normal_matrix + damping * jnp.eye(DATES - 1, dtype=jnp.float32)
    factor = jnp.linalg.cholesky(normal_matrix)
    inverse = jax.scipy.linalg.cho_solve((factor, True), design.T)
    return (design, inverse)


def pooling_matrix():
    row = lax.broadcasted_iota(jnp.int32, (LANES * RG_LOOKS, LANES), 0)
    col = lax.broadcasted_iota(jnp.int32, (LANES * RG_LOOKS, LANES), 1)
    return (row // RG_LOOKS == col).astype(jnp.bfloat16)


def horner(coefficients, z):
    total = coefficients[-1] * z + coefficients[-2]
    for c in coefficients[-3::-1]:
        total = total * z + c
    return total


def regroup(ref, held, rows):
    held[...] = ref[rows].astype(jnp.float32).reshape(GROUP * PIECES, LANES)


def piece(held, q):
    return held[pl.ds(q, GROUP, stride=PIECES), :]


def split_store(high, low, rows, c, value):
    top = value.astype(jnp.bfloat16)
    high[rows, c * LANES : (c + 1) * LANES] = top
    low[rows, c * LANES : (c + 1) * LANES] = (value - top.astype(jnp.float32)).astype(jnp.bfloat16)


def pooled(high, low, pool):
    return jnp.dot(high[...], pool[...], preferred_element_type=jnp.float32) + jnp.dot(
        low[...], pool[...], preferred_element_type=jnp.float32
    )


def phase_kernel(phase, weight, pool, look_weight, looked, p_held, w_held, wh, wl, ph, plo):
    block = phase.shape[0]

    def step(g, carry):
        rows = pl.ds(pl.multiple_of(g * GROUP, GROUP), GROUP)
        regroup(phase, p_held, rows)
        regroup(weight, w_held, rows)
        for c in range(RG_LOOKS):
            w0, w1 = piece(w_held, 2 * c), piece(w_held, 2 * c + 1)
            p0, p1 = piece(p_held, 2 * c), piece(p_held, 2 * c + 1)
            split_store(wh, wl, rows, c, w0 + w1)
            split_store(ph, plo, rows, c, w0 * p0 + w1 * p1)
        return carry

    lax.fori_loop(0, block // GROUP, step, 0)
    total = pooled(wh, wl, pool)
    look_weight[...] = total
    mean = pooled(ph, plo, pool) / total
    looked[...] = jnp.transpose(mean.reshape(block // 32, 4, 8, LANES), (1, 0, 2, 3))


def phase_looks(phase, weight, pool):
    rows = phase.shape[0]
    block = 480
    return pl.pallas_call(
        phase_kernel,
        grid=(rows // block,),
        in_specs=[
            pl.BlockSpec((block, PIECES, LANES), lambda i: (i, 0, 0)),
            pl.BlockSpec((block, PIECES, LANES), lambda i: (i, 0, 0)),
            pl.BlockSpec(pool.shape, lambda i: (0, 0)),
        ],
        out_specs=[
            pl.BlockSpec((block, LANES), lambda i: (i, 0)),
            pl.BlockSpec((4, block // 32, 8, LANES), lambda i: (0, i, 0, 0)),
        ],
        out_shape=[
            jax.ShapeDtypeStruct((rows, LANES), jnp.float32),
            jax.ShapeDtypeStruct((4, rows // 32, 8, LANES), jnp.float32),
        ],
        scratch_shapes=[pltpu.VMEM((GROUP * PIECES, LANES), jnp.float32)] * 2
        + [pltpu.VMEM((block, RG_LOOKS * LANES), jnp.bfloat16)] * 4,
        compiler_params=pltpu.CompilerParams(vmem_limit_bytes=48 * 1024 * 1024),
        cost_estimate=pl.CostEstimate(
            flops=2 * rows * 2048 * 128, bytes_accessed=2 * rows * 4096 + rows * 1024, transcendentals=0
        ),
        name="phase_looks",
    )(phase, weight, pool)


def wave_kernel(start, phase, weight, pool, look_weight, out, p_held, w_held, sh, sl, qh, ql):
    block = phase.shape[0]

    def step(g, carry):
        rows = pl.ds(pl.multiple_of(g * GROUP, GROUP), GROUP)
        regroup(phase, p_held, rows)
        regroup(weight, w_held, rows)
        for c in range(RG_LOOKS):
            s_sum = q_sum = None
            for a in range(AZ_LOOKS):
                x = piece(p_held, 2 * c + a)
                w = piece(w_held, 2 * c + a)
                z = x * x
                s = x * horner(SIN_QUARTER, z)
                k = horner(COS_QUARTER, z)
                half = s * k
                sine = w * (half * (1.0 - s * s))
                versed = w * (half * half)
                s_sum = sine if s_sum is None else s_sum + sine
                q_sum = versed if q_sum is None else q_sum + versed
            split_store(sh, sl, rows, c, s_sum)
            split_store(qh, ql, rows, c, q_sum)
        return carry

    lax.fori_loop(0, block // GROUP, step, 0)
    out[0] = look_weight[...] - 4.0 * pooled(qh, ql, pool)
    out[1] = SIN_SCALE * pooled(sh, sl, pool)


def wave_looks(start, count, phase, weight, pool, look_weight):
    block = 304
    element = pl.Element
    return pl.pallas_call(
        wave_kernel,
        grid_spec=pltpu.PrefetchScalarGridSpec(
            num_scalar_prefetch=1,
            grid=(count // block,),
            in_specs=[
                pl.BlockSpec(
                    (element(block), element(PIECES), element(LANES)),
                    lambda i, s: (pl.multiple_of(s[0] + i * block, 16), 0, 0),
                ),
                pl.BlockSpec(
                    (element(block), element(PIECES), element(LANES)),
                    lambda i, s: (pl.multiple_of(s[0] + i * block, 16), 0, 0),
                ),
                pl.BlockSpec(pool.shape, lambda i, s: (0, 0)),
                pl.BlockSpec(
                    (element(block), element(LANES)),
                    lambda i, s: (pl.multiple_of(s[0] + i * block, 16), 0),
                ),
            ],
            out_specs=pl.BlockSpec((2, block, LANES), lambda i, s: (0, i, 0)),
            scratch_shapes=[pltpu.VMEM((GROUP * PIECES, LANES), jnp.float32)] * 2
            + [pltpu.VMEM((block, RG_LOOKS * LANES), jnp.bfloat16)] * 4,
        ),
        out_shape=jax.ShapeDtypeStruct((2, count, LANES), jnp.float32),
        compiler_params=pltpu.CompilerParams(vmem_limit_bytes=48 * 1024 * 1024),
        cost_estimate=pl.CostEstimate(
            flops=40 * count * 2048, bytes_accessed=2 * count * 4096 + count * 1024, transcendentals=0
        ),
        name="wave_looks",
    )(start, phase, weight, pool, look_weight)


def window_kernel(
    row_off, col_off, flip, own_cs, own_w, mate_cs, mate_w, near_cs, near_w, far_cs, far_w,
    own_out, mate_out, held, cre, cim, sems,
):
    copies = []
    for i, (cs, w) in enumerate(
        ((near_cs, near_w), (own_cs, own_w), (mate_cs, mate_w), (far_cs, far_w))
    ):
        copies.append(pltpu.make_async_copy(cs, held.at[i, pl.ds(0, 2)], sems.at[i, 0]))
        copies.append(pltpu.make_async_copy(w, held.at[i, 2], sems.at[i, 1]))
    for c in copies:
        c.start()
    for c in copies:
        c.wait()
    cols = held.shape[2] // 32
    lane = lax.broadcasted_iota(jnp.int32, (8, LANES), 1)
    shifts = [col_off[k] for k in range(OFFSETS)]
    rolls = [lax.rem(LANES - d, LANES) for d in shifts]
    groups = (cols + 7) // 8

    def one(t, carry):
        side, g = t // groups, lax.rem(t, groups)
        first = jnp.minimum(g * 8, cols - 8) * 32
        sources = [1 + side + row_off[k] * flip[0] for k in range(OFFSETS)]
        after = [lane + d >= LANES for d in shifts]
        before = [lane + d < 0 for d in shifts]
        for quantity in range(3):
            def rolled(c):
                if c < 0 or c > 31:
                    return [jnp.zeros((8, LANES), jnp.float32)] * OFFSETS
                out = []
                for k in range(OFFSETS):
                    v = held[sources[k], quantity, pl.ds(first + c, 8, stride=32), :]
                    out.append(pltpu.roll(v, rolls[k], 1))
                return out

            last, now = rolled(-1), rolled(0)
            for c in range(32):
                following = rolled(c + 1)
                total = None
                for k in range(OFFSETS):
                    term = jnp.where(after[k], following[k], jnp.where(before[k], last[k], now[k]))
                    total = term if total is None else total + term
                last, now = now, following
                if quantity == 0:
                    cre[c] = total
                elif quantity == 1:
                    cim[c] = total
                else:
                    re, im = cre[c], cim[c]
                    value = jnp.sqrt(re * re + im * im) / total
                    @pl.when(side == 0)
                    def _():
                        own_out[pl.ds(first + c, 8, stride=32), :] = value
                    @pl.when(side == 1)
                    def _():
                        mate_out[pl.ds(first + c, 8, stride=32), :] = value
        return carry

    lax.fori_loop(0, 2 * groups, one, 0)


def window_coherence(row_off, col_off, flip, own_cs, own_w, mate_cs, mate_w, near_cs, near_w, far_cs, far_w):
    rows = own_w.shape[0]
    smem = pl.BlockSpec(memory_space=pltpu.SMEM)
    hbm = pl.BlockSpec(memory_space=pl.ANY)
    vmem = pl.BlockSpec(memory_space=pltpu.VMEM)
    shape = jax.ShapeDtypeStruct((rows, LANES), jnp.float32)
    return pl.pallas_call(
        window_kernel,
        in_specs=[smem] * 3 + [hbm] * 8,
        out_specs=[vmem, vmem],
        out_shape=[shape, shape],
        scratch_shapes=[
            pltpu.VMEM((4, 3, rows, LANES), jnp.float32),
            pltpu.VMEM((32, 8, LANES), jnp.float32),
            pltpu.VMEM((32, 8, LANES), jnp.float32),
            pltpu.SemaphoreType.DMA((4, 2)),
        ],
        compiler_params=pltpu.CompilerParams(vmem_limit_bytes=32 * 1024 * 1024),
        cost_estimate=pl.CostEstimate(
            flops=200 * rows * LANES, bytes_accessed=14 * rows * LANES * 4, transcendentals=0
        ),
        name="window_coherence",
    )(row_off, col_off, flip, own_cs, own_w, mate_cs, mate_w, near_cs, near_w, far_cs, far_w)


def invert_kernel(looked, inverse, design, residual, history, flat):
    ifgs = design.shape[0]
    for j in range(8):
        flat[:, j * LANES : (j + 1) * LANES] = looked[pl.ds(j, ifgs, stride=8), :]
    phase = flat[...]
    solved = jnp.dot(
        inverse[...], phase, precision=lax.Precision.HIGHEST, preferred_element_type=jnp.float32
    )
    fitted = jnp.dot(
        design[...], solved, precision=lax.Precision.HIGHEST, preferred_element_type=jnp.float32
    )
    history[...] = jnp.transpose(solved)[:, : DATES - 1]
    rest = phase - fitted
    for j in range(8):
        residual[pl.ds(j, ifgs, stride=8), :] = rest[:, j * LANES : (j + 1) * LANES]


def invert(looked, inverse, design):
    ifgs = design.shape[0]
    vmem = pl.BlockSpec(memory_space=pltpu.VMEM)
    return pl.pallas_call(
        invert_kernel,
        in_specs=[vmem] * 3,
        out_specs=[vmem] * 2,
        out_shape=[
            jax.ShapeDtypeStruct(looked.shape, jnp.float32),
            jax.ShapeDtypeStruct((8 * LANES, DATES - 1), jnp.float32),
        ],
        scratch_shapes=[pltpu.VMEM((ifgs, 8 * LANES), jnp.float32)],
        compiler_params=pltpu.CompilerParams(vmem_limit_bytes=32 * 1024 * 1024),
        cost_estimate=pl.CostEstimate(
            flops=24 * ifgs * DATES * 1024, bytes_accessed=4 * 3 * ifgs * 1024, transcendentals=0
        ),
        name="invert",
    )(looked, inverse, design)


def tiles(samples):
    ifgs, az, cols = samples.shape
    split = samples.reshape(ifgs, az, cols // LANES, LANES).transpose(0, 2, 1, 3)
    return split.reshape(ifgs * cols // (LANES * RG_LOOKS), PIECES, LANES)


def local(phase_samples, sample_weights, reference_date, secondary_date, window_rows, window_cols):
    ifgs = phase_samples.shape[0]
    row_count = lax.axis_size("rows")
    odd = lax.rem(lax.axis_index("rows"), 2)
    share = (ifgs + 1) // 2
    rest = ifgs - share
    mates = [(r, r ^ 1) for r in range(row_count)]
    outward = [(r, r + 2 if r % 2 else r - 2) for r in range(row_count)]
    outward = [(s, d) for s, d in outward if 0 <= d < row_count]
    across = [(r, r - 2 if r % 2 else r + 2) for r in range(row_count)]
    across = [(s, d) for s, d in across if 0 <= d < row_count]

    phase = tiles(phase_samples)
    weight = tiles(sample_weights)
    pool = pooling_matrix()
    look_weight, looked = phase_looks(phase, weight, pool)
    moved = lax.all_to_all(looked, "ifg", split_axis=0, concat_axis=0, tiled=True)

    mine = rest * 32 * odd
    other = rest * 32 * (1 - odd)
    size = share * 32
    own_w = lax.dynamic_slice_in_dim(look_weight, mine, size)
    sent_w = lax.dynamic_slice_in_dim(look_weight, other, size)
    mate_w = lax.ppermute(sent_w, "rows", mates)
    sent_cs = wave_looks(other.reshape(1), size, phase, weight, pool, look_weight)
    mate_cs = lax.ppermute(sent_cs, "rows", mates)
    own_cs = wave_looks(mine.reshape(1), size, phase, weight, pool, look_weight)
    far_w = lax.ppermute(own_w, "rows", outward)
    far_cs = lax.ppermute(own_cs, "rows", outward)
    near_w = lax.ppermute(mate_w, "rows", across)
    near_cs = lax.ppermute(mate_cs, "rows", across)
    flip = (1 - 2 * odd).reshape(1)
    own_part, mate_part = window_coherence(
        window_rows, window_cols, flip, own_cs, own_w, mate_cs, mate_w, near_cs, near_w, far_cs, far_w
    )
    back = lax.ppermute(mate_part, "rows", mates)
    extra = (share - rest) * 32
    coherence = jnp.where(
        odd == 0,
        jnp.concatenate([own_part, back[extra:]]),
        jnp.concatenate([back, own_part[extra:]]),
    )

    design, inverse = network_solve(reference_date, secondary_date)
    tile_rows = moved.shape[0] * moved.shape[1] * moved.shape[2]
    residual, history = invert(moved.reshape(tile_rows, LANES), inverse, design)
    residual = lax.all_to_all(
        residual.reshape(moved.shape), "ifg", split_axis=0, concat_axis=0, tiled=True
    )
    residual = residual.transpose(1, 0, 2, 3)
    history = history.reshape(row_count, -1, DATES - 1)
    history = lax.all_to_all(history, "rows", split_axis=0, concat_axis=0, tiled=True)
    shape = (ifgs, 1, 32 * LANES)
    return (coherence.reshape(shape), residual.reshape(shape), history.transpose(2, 0, 1))


def solution(mesh):
    placed = (P("ifg", "rows", None), P("ifg", "rows", None), P(), P(), P(), P())
    return jax.shard_map(
        local,
        mesh=mesh,
        in_specs=placed,
        out_specs=(P("ifg", "rows", None), P("ifg", "rows", None), P(None, None, ("ifg", "rows"))),
        check_vma=False,
    )
```

```python
import math

import jax
import jax.numpy as jnp
from jax import lax
from jax.experimental import pallas as pl
from jax.experimental.pallas import tpu as pltpu
from jax.sharding import PartitionSpec as P

DATES = 160
AZ_LOOKS = 2
RG_LOOKS = 8
REACH = 24
OFFSETS = 9
LANES = 128

damping = 0.25

SIN_QUARTER = (
    0.3535533845424652,
    -0.0036828448064625263,
    1.1508434909046628e-05,
    -1.7096880355893518e-08,
    1.4046378643550739e-11,
)
COS_QUARTER = (
    0.9999999403953552,
    -0.031249957159161568,
    0.00016275106463581324,
    -3.383578359716921e-07,
    3.553040917037009e-10,
)
SIN_SCALE = 2.0 * math.sqrt(2.0)

PIECES = 16
PITCH = 17
GROUP = 16


def pooling_matrix():
    row = lax.broadcasted_iota(jnp.int32, (LANES * RG_LOOKS, LANES), 0)
    col = lax.broadcasted_iota(jnp.int32, (LANES * RG_LOOKS, LANES), 1)
    return (row // RG_LOOKS == col).astype(jnp.bfloat16)


def horner(coefficients, z):
    total = coefficients[-1] * z + coefficients[-2]
    for c in coefficients[-3::-1]:
        total = total * z + c
    return total


def regroup(ref, held, rows):
    tiles = ref[rows].astype(jnp.float32)
    for m in range(GROUP):
        held[m * PITCH : m * PITCH + PIECES, :] = tiles[m]


def piece(held, q):
    return held[pl.ds(q, GROUP, stride=PITCH), :]


def split_store(high, low, rows, c, value):
    top = value.astype(jnp.bfloat16)
    high[rows, c * LANES : (c + 1) * LANES] = top
    low[rows, c * LANES : (c + 1) * LANES] = (value - top.astype(jnp.float32)).astype(jnp.bfloat16)


def pooled(high, low, pool):
    return jnp.dot(high[...], pool[...], preferred_element_type=jnp.float32) + jnp.dot(
        low[...], pool[...], preferred_element_type=jnp.float32
    )


def phase_kernel(phase, weight, pool, look_weight, looked, p_held, w_held, wh, wl, ph, plo):
    block = phase.shape[0]

    def step(g, carry):
        rows = pl.ds(pl.multiple_of(g * GROUP, GROUP), GROUP)
        regroup(phase, p_held, rows)
        regroup(weight, w_held, rows)
        for c in range(RG_LOOKS):
            w0, w1 = piece(w_held, 2 * c), piece(w_held, 2 * c + 1)
            p0, p1 = piece(p_held, 2 * c), piece(p_held, 2 * c + 1)
            split_store(wh, wl, rows, c, w0 + w1)
            split_store(ph, plo, rows, c, w0 * p0 + w1 * p1)
        return carry

    lax.fori_loop(0, block // GROUP, step, 0)
    total = pooled(wh, wl, pool)
    look_weight[...] = total
    mean = pooled(ph, plo, pool) / total
    looked[...] = jnp.transpose(mean.reshape(block // 32, 4, 8, LANES), (1, 0, 2, 3))


def phase_looks(phase, weight, pool):
    rows = phase.shape[0]
    block = 480
    return pl.pallas_call(
        phase_kernel,
        grid=(rows // block,),
        in_specs=[
            pl.BlockSpec((block, PIECES, LANES), lambda i: (i, 0, 0)),
            pl.BlockSpec((block, PIECES, LANES), lambda i: (i, 0, 0)),
            pl.BlockSpec(pool.shape, lambda i: (0, 0)),
        ],
        out_specs=[
            pl.BlockSpec((block, LANES), lambda i: (i, 0)),
            pl.BlockSpec((4, block // 32, 8, LANES), lambda i: (0, i, 0, 0)),
        ],
        out_shape=[
            jax.ShapeDtypeStruct((rows, LANES), jnp.float32),
            jax.ShapeDtypeStruct((4, rows // 32, 8, LANES), jnp.float32),
        ],
        scratch_shapes=[pltpu.VMEM((GROUP * PITCH, LANES), jnp.float32)] * 2
        + [pltpu.VMEM((block, RG_LOOKS * LANES), jnp.bfloat16)] * 4,
        compiler_params=pltpu.CompilerParams(vmem_limit_bytes=48 * 1024 * 1024),
        cost_estimate=pl.CostEstimate(
            flops=2 * rows * 2048 * 128, bytes_accessed=2 * rows * 4096 + rows * 1024, transcendentals=0
        ),
        name="phase_looks",
    )(phase, weight, pool)


def wave_kernel(start, phase, weight, pool, look_weight, out, p_held, w_held, sh, sl, qh, ql):
    block = phase.shape[0]

    def step(g, carry):
        rows = pl.ds(pl.multiple_of(g * GROUP, GROUP), GROUP)
        regroup(phase, p_held, rows)
        regroup(weight, w_held, rows)
        for c in range(RG_LOOKS):
            s_sum = q_sum = None
            for a in range(AZ_LOOKS):
                x = piece(p_held, 2 * c + a)
                w = piece(w_held, 2 * c + a)
                z = x * x
                s = x * horner(SIN_QUARTER, z)
                k = horner(COS_QUARTER, z)
                half = s * k
                sine = w * (half * (1.0 - s * s))
                versed = w * (half * half)
                s_sum = sine if s_sum is None else s_sum + sine
                q_sum = versed if q_sum is None else q_sum + versed
            split_store(sh, sl, rows, c, s_sum)
            split_store(qh, ql, rows, c, q_sum)
        return carry

    lax.fori_loop(0, block // GROUP, step, 0)
    out[0] = look_weight[...] - 4.0 * pooled(qh, ql, pool)
    out[1] = SIN_SCALE * pooled(sh, sl, pool)


def wave_looks(start, count, phase, weight, pool, look_weight):
    block = 304
    element = pl.Element
    return pl.pallas_call(
        wave_kernel,
        grid_spec=pltpu.PrefetchScalarGridSpec(
            num_scalar_prefetch=1,
            grid=(count // block,),
            in_specs=[
                pl.BlockSpec(
                    (element(block), element(PIECES), element(LANES)),
                    lambda i, s: (pl.multiple_of(s[0] + i * block, 16), 0, 0),
                ),
                pl.BlockSpec(
                    (element(block), element(PIECES), element(LANES)),
                    lambda i, s: (pl.multiple_of(s[0] + i * block, 16), 0, 0),
                ),
                pl.BlockSpec(pool.shape, lambda i, s: (0, 0)),
                pl.BlockSpec(
                    (element(block), element(LANES)),
                    lambda i, s: (pl.multiple_of(s[0] + i * block, 16), 0),
                ),
            ],
            out_specs=pl.BlockSpec((2, block, LANES), lambda i, s: (0, i, 0)),
            scratch_shapes=[pltpu.VMEM((GROUP * PITCH, LANES), jnp.float32)] * 2
            + [pltpu.VMEM((block, RG_LOOKS * LANES), jnp.bfloat16)] * 4,
        ),
        out_shape=jax.ShapeDtypeStruct((2, count, LANES), jnp.float32),
        compiler_params=pltpu.CompilerParams(vmem_limit_bytes=48 * 1024 * 1024),
        cost_estimate=pl.CostEstimate(
            flops=40 * count * 2048, bytes_accessed=2 * count * 4096 + count * 1024, transcendentals=0
        ),
        name="wave_looks",
    )(start, phase, weight, pool, look_weight)


def window_kernel(
    near_cs, near_w, own_cs, own_w, mate_cs, mate_w, far_cs, far_w, bands, own_out, mate_out, parts
):
    rows = own_w.shape[0]
    pairs = ((near_cs, near_w), (own_cs, own_w), (mate_cs, mate_w), (far_cs, far_w))

    def divide(g, carry):
        r = pl.ds(pl.multiple_of(g * 32, 32), 32)
        for source, (cs, w) in enumerate(pairs):
            for quantity in range(3):
                value = cs[quantity, r, :] if quantity < 2 else w[r, :]
                high = value.astype(jnp.bfloat16)
                low = (value - high.astype(jnp.float32)).astype(jnp.bfloat16)
                at = source * 2 * LANES
                parts[quantity, r, at : at + LANES] = high
                parts[quantity, r, at + LANES : at + 2 * LANES] = low
        return carry

    lax.fori_loop(0, rows // 32, divide, 0)
    lane = lax.broadcasted_iota(jnp.int32, (rows, LANES), 1)
    row = lax.rem(lax.broadcasted_iota(jnp.int32, (rows, LANES), 0), 32)
    upper = lane >= LANES // 2
    valid = (upper & (row < 31)) | (jnp.logical_not(upper) & (row > 0))
    for side, out in enumerate((own_out, mate_out)):
        sums = []
        for quantity in range(3):
            left = parts[quantity, :, side * 2 * LANES : (side + 3) * 2 * LANES]
            both = jnp.dot(left, bands[...], preferred_element_type=jnp.float32)
            edge = both[:, LANES:]
            edge = jnp.where(upper, pltpu.roll(edge, rows - 1, 0), pltpu.roll(edge, 1, 0))
            sums.append(both[:, :LANES] + jnp.where(valid, edge, 0.0))
        re, im, w = sums
        out[...] = jnp.sqrt(re * re + im * im) / w


def window_coherence(bands, own_cs, own_w, mate_cs, mate_w, near_cs, near_w, far_cs, far_w):
    rows = own_w.shape[0]
    block = rows // 2
    cs = pl.BlockSpec((2, block, LANES), lambda i: (0, i, 0))
    w = pl.BlockSpec((block, LANES), lambda i: (i, 0))
    shape = jax.ShapeDtypeStruct((rows, LANES), jnp.float32)
    return pl.pallas_call(
        window_kernel,
        grid=(2,),
        in_specs=[cs, w] * 4 + [pl.BlockSpec(bands.shape, lambda i: (0, 0))],
        out_specs=[w, w],
        out_shape=[shape, shape],
        scratch_shapes=[pltpu.VMEM((3, block, 8 * LANES), jnp.bfloat16)],
        compiler_params=pltpu.CompilerParams(vmem_limit_bytes=40 * 1024 * 1024),
        cost_estimate=pl.CostEstimate(
            flops=6 * rows * 768 * 512, bytes_accessed=14 * rows * LANES * 4, transcendentals=0
        ),
        name="window_coherence",
    )(near_cs, near_w, own_cs, own_w, mate_cs, mate_w, far_cs, far_w, bands)


def window_bands(row_off, col_off, flip, bands):
    gap = lax.broadcasted_iota(jnp.int32, (LANES, LANES), 1) - lax.broadcasted_iota(
        jnp.int32, (LANES, LANES), 0
    )
    for e in range(3):
        same = jnp.zeros((LANES, LANES), jnp.float32)
        next_to = jnp.zeros((LANES, LANES), jnp.float32)
        for k in range(OFFSETS):
            amount = jnp.where(row_off[k] * flip[0] == e - 1, 1.0, 0.0)
            moved = gap + col_off[k]
            same = same + jnp.where(moved == 0, amount, 0.0)
            next_to = next_to + jnp.where(jnp.abs(moved) == LANES, amount, 0.0)
        for half in range(2):
            rows = slice((2 * e + half) * LANES, (2 * e + half + 1) * LANES)
            bands[rows, :LANES] = same.astype(jnp.bfloat16)
            bands[rows, LANES:] = next_to.astype(jnp.bfloat16)


def network_kernel(
    row_off, col_off, flip, reference, secondary, inverse, design, bands, grid
):
    count = inverse.shape[0]
    window_bands(row_off, col_off, flip, bands)
    date = lax.broadcasted_iota(jnp.int32, inverse.shape, 0) + 1
    signed = (secondary[...] == date).astype(jnp.float32) - (reference[...] == date).astype(jnp.float32)
    design[...] = jnp.transpose(signed)
    exact = signed.astype(jnp.bfloat16)
    normal = lax.dot_general(
        exact, exact, (((1,), (1,)), ((), ())), preferred_element_type=jnp.float32
    )
    i = lax.broadcasted_iota(jnp.int32, (count, count), 0)
    j = lax.broadcasted_iota(jnp.int32, (count, count), 1)
    normal = normal + jnp.where(i == j, jnp.where(i == DATES - 1, 1.0, damping), 0.0)
    grid[0] = normal[:, :LANES]
    grid[1] = jnp.zeros((count, LANES), jnp.float32)
    grid[1, :, : count - LANES] = normal[:, LANES:]
    lane = lax.broadcasted_iota(jnp.int32, (1, LANES), 1)
    for first in range(0, count, 32):
        rows = min(first + 32 + REACH, count)
        tiles = range(1 if rows <= LANES else 2)
        half = first // LANES

        def sweep(k, carry):
            here = k - half * LANES
            picked = lane == here
            lines = [grid[t, pl.ds(k, 1), :] for t in tiles]
            values = [grid[t, :rows, :] for t in tiles]
            scale = 1.0 / jnp.sum(jnp.where(picked, lines[half], 0.0), axis=1, keepdims=True)
            lines = [line * scale for line in lines]
            lines[half] = jnp.where(picked, -scale, lines[half])
            index = jnp.full((rows, LANES), here, jnp.int32)
            column = jnp.take_along_axis(values[half], index, axis=1)
            values[half] = jnp.where(picked, 0.0, values[half])
            for t in tiles:
                grid[t, :rows, :] = values[t] - column * lines[t]
            for t in tiles:
                grid[t, pl.ds(k, 1), :] = lines[t]
            return carry

        lax.fori_loop(first, first + 32, sweep, 0)
    swept = jnp.concatenate([grid[0], grid[1, :, : count - LANES]], axis=1)
    inverse[...] = -jnp.dot(
        swept, signed, precision=lax.Precision.HIGHEST, preferred_element_type=jnp.float32
    )


def network_solve(window_rows, window_cols, flip, reference_date, secondary_date):
    pairs = reference_date.shape[0]
    vmem = pl.BlockSpec(memory_space=pltpu.VMEM)
    smem = pl.BlockSpec(memory_space=pltpu.SMEM)
    return pl.pallas_call(
        network_kernel,
        in_specs=[smem] * 3 + [vmem] * 2,
        out_specs=[vmem] * 3,
        out_shape=[
            jax.ShapeDtypeStruct((DATES, pairs), jnp.float32),
            jax.ShapeDtypeStruct((pairs, DATES), jnp.float32),
            jax.ShapeDtypeStruct((6 * LANES, 2 * LANES), jnp.bfloat16),
        ],
        scratch_shapes=[pltpu.VMEM((2, DATES, LANES), jnp.float32)],
        compiler_params=pltpu.CompilerParams(vmem_limit_bytes=16 * 1024 * 1024),
        cost_estimate=pl.CostEstimate(
            flops=20_000_000, bytes_accessed=80_000_000, transcendentals=0
        ),
        name="network_solve",
    )(window_rows, window_cols, flip, reference_date[None, :], secondary_date[None, :])


def invert_kernel(looked, inverse, design, residual, history, flat):
    ifgs = design.shape[0]
    for j in range(8):
        flat[:, j * LANES : (j + 1) * LANES] = looked[pl.ds(j, ifgs, stride=8), :]
    phase = flat[...]

    def product(a, b):
        return jnp.dot(a, b, precision=lax.Precision.HIGHEST, preferred_element_type=jnp.float32)

    solved = product(inverse[...], phase)
    history[...] = jnp.transpose(solved)[:, : DATES - 1]
    rest = phase - product(design[...], solved)
    for j in range(8):
        residual[pl.ds(j, ifgs, stride=8), :] = rest[:, j * LANES : (j + 1) * LANES]


def invert(looked, inverse, design):
    ifgs = design.shape[0]
    vmem = pl.BlockSpec(memory_space=pltpu.VMEM)
    return pl.pallas_call(
        invert_kernel,
        in_specs=[vmem] * 3,
        out_specs=[vmem] * 2,
        out_shape=[
            jax.ShapeDtypeStruct(looked.shape, jnp.float32),
            jax.ShapeDtypeStruct((8 * LANES, DATES - 1), jnp.float32),
        ],
        scratch_shapes=[pltpu.VMEM((ifgs, 8 * LANES), jnp.float32)],
        compiler_params=pltpu.CompilerParams(vmem_limit_bytes=32 * 1024 * 1024),
        cost_estimate=pl.CostEstimate(
            flops=24 * ifgs * DATES * 1024, bytes_accessed=4 * 3 * ifgs * 1024, transcendentals=0
        ),
        name="invert",
    )(looked, inverse, design)


def tiles(samples):
    ifgs, az, cols = samples.shape
    split = samples.reshape(ifgs, az, cols // LANES, LANES).transpose(0, 2, 1, 3)
    return split.reshape(ifgs * cols // (LANES * RG_LOOKS), PIECES, LANES)


def local(phase_samples, sample_weights, reference_date, secondary_date, window_rows, window_cols):
    ifgs = phase_samples.shape[0]
    row_count = lax.axis_size("rows")
    odd = lax.rem(lax.axis_index("rows"), 2)
    share = (ifgs + 1) // 2
    rest = ifgs - share
    mates = [(r, r ^ 1) for r in range(row_count)]
    outward = [(r, r + 2 if r % 2 else r - 2) for r in range(row_count)]
    outward = [(s, d) for s, d in outward if 0 <= d < row_count]
    across = [(r, r - 2 if r % 2 else r + 2) for r in range(row_count)]
    across = [(s, d) for s, d in across if 0 <= d < row_count]

    phase = tiles(phase_samples)
    weight = tiles(sample_weights)
    pool = pooling_matrix()
    flip = (1 - 2 * odd).reshape(1)
    inverse, design, bands = network_solve(
        window_rows, window_cols, flip, reference_date, secondary_date
    )
    look_weight, looked = phase_looks(phase, weight, pool)
    moved = lax.all_to_all(looked, "ifg", split_axis=0, concat_axis=0, tiled=True)

    mine = rest * 32 * odd
    other = rest * 32 * (1 - odd)
    size = share * 32
    own_w = lax.dynamic_slice_in_dim(look_weight, mine, size)
    sent_w = lax.dynamic_slice_in_dim(look_weight, other, size)
    mate_w = lax.ppermute(sent_w, "rows", mates)
    sent_cs = wave_looks(other.reshape(1), size, phase, weight, pool, look_weight)
    mate_cs = lax.ppermute(sent_cs, "rows", mates)
    own_cs = wave_looks(mine.reshape(1), size, phase, weight, pool, look_weight)
    far_w = lax.ppermute(own_w, "rows", outward)
    far_cs = lax.ppermute(own_cs, "rows", outward)
    near_w = lax.ppermute(mate_w, "rows", across)
    near_cs = lax.ppermute(mate_cs, "rows", across)
    own_part, mate_part = window_coherence(
        bands, own_cs, own_w, mate_cs, mate_w, near_cs, near_w, far_cs, far_w
    )
    back = lax.ppermute(mate_part, "rows", mates)
    extra = (share - rest) * 32
    coherence = jnp.where(
        odd == 0,
        jnp.concatenate([own_part, back[extra:]]),
        jnp.concatenate([back, own_part[extra:]]),
    )

    tile_rows = moved.shape[0] * moved.shape[1] * moved.shape[2]
    residual, history = invert(moved.reshape(tile_rows, LANES), inverse, design)
    residual = lax.all_to_all(
        residual.reshape(moved.shape), "ifg", split_axis=0, concat_axis=0, tiled=True
    )
    residual = residual.transpose(1, 0, 2, 3)
    history = history.reshape(row_count, -1, DATES - 1)
    history = lax.all_to_all(history, "rows", split_axis=0, concat_axis=0, tiled=True)
    shape = (ifgs, 1, 32 * LANES)
    return (coherence.reshape(shape), residual.reshape(shape), history.transpose(2, 0, 1))


def solution(mesh):
    placed = (P("ifg", "rows", None), P("ifg", "rows", None), P(), P(), P(), P())
    return jax.shard_map(
        local,
        mesh=mesh,
        in_specs=placed,
        out_specs=(P("ifg", "rows", None), P("ifg", "rows", None), P(None, None, ("ifg", "rows"))),
        check_vma=False,
    )
```

```python
import functools
import math

import jax
import jax.numpy as jnp
from jax import lax
from jax.experimental import pallas as pl
from jax.experimental.pallas import tpu as pltpu
from jax.sharding import PartitionSpec as P

DATES = 160
AZ_LOOKS = 2
RG_LOOKS = 8
REACH = 24
OFFSETS = 9
LANES = 128

damping = 0.25

SIN_QUARTER = (
    0.3535533845424652,
    -0.0036828448064625263,
    1.1508434909046628e-05,
    -1.7096880355893518e-08,
    1.4046378643550739e-11,
)
COS_QUARTER = (
    0.9999999403953552,
    -0.031249957159161568,
    0.00016275106463581324,
    -3.383578359716921e-07,
    3.553040917037009e-10,
)
SIN_SCALE = 2.0 * math.sqrt(2.0)

PIECES = 16
PITCH = 17
GROUPS = 4
FIRST = 20
GROUP = 16


def pooling_matrix():
    row = lax.broadcasted_iota(jnp.int32, (LANES * RG_LOOKS, LANES), 0)
    col = lax.broadcasted_iota(jnp.int32, (LANES * RG_LOOKS, LANES), 1)
    return (row // RG_LOOKS == col).astype(jnp.bfloat16)


def lasting(us):
    return pl.CostEstimate(flops=0, bytes_accessed=int(us * 3.6e6), transcendentals=0)


def horner(coefficients, z):
    total = coefficients[-1] * z + coefficients[-2]
    for c in coefficients[-3::-1]:
        total = total * z + c
    return total


def regroup(ref, held, rows):
    tiles = ref[rows].astype(jnp.float32)
    for m in range(GROUP):
        held[m * PITCH : m * PITCH + PIECES, :] = tiles[m]


def piece(held, q):
    return held[pl.ds(q, GROUP, stride=PITCH), :]


def split_store(high, low, rows, c, value):
    top = value.astype(jnp.bfloat16)
    high[rows, c * LANES : (c + 1) * LANES] = top
    low[rows, c * LANES : (c + 1) * LANES] = (value - top.astype(jnp.float32)).astype(jnp.bfloat16)


def pooled(high, low, pool):
    return jnp.dot(high[...], pool[...], preferred_element_type=jnp.float32) + jnp.dot(
        low[...], pool[...], preferred_element_type=jnp.float32
    )


def look_kernel(start, phase, weight, pool, *refs):
    out, looked, p_held, w_held, wh, wl, ph, plo, sh, sl, qh, ql = refs[-12:]
    block = phase.shape[0]

    def step(g, carry):
        rows = pl.ds(pl.multiple_of(g * GROUP, GROUP), GROUP)
        regroup(phase, p_held, rows)
        regroup(weight, w_held, rows)
        for c in range(RG_LOOKS):
            sums = None
            for a in range(AZ_LOOKS):
                x = piece(p_held, 2 * c + a)
                w = piece(w_held, 2 * c + a)
                z = x * x
                s = x * horner(SIN_QUARTER, z)
                k = horner(COS_QUARTER, z)
                half = s * k
                terms = (w, w * x, w * (half * (1.0 - s * s)), w * (half * half))
                sums = terms if sums is None else [t + u for t, u in zip(sums, terms)]
            for value, high, low in zip(sums, (wh, ph, sh, qh), (wl, plo, sl, ql)):
                split_store(high, low, rows, c, value)
        return carry

    lax.fori_loop(0, block // GROUP, step, 0)
    total = pooled(wh, wl, pool)
    mean = pooled(ph, plo, pool) / total
    looked[...] = jnp.transpose(mean.reshape(block // 32, GROUPS, 8, LANES), (1, 0, 2, 3))
    out[0] = total - 4.0 * pooled(qh, ql, pool)
    out[1] = SIN_SCALE * pooled(sh, sl, pool)
    out[2] = total


def look_sums(start, count, block, slot, slots, phase, weight, pool, looked=None, after=()):
    element = pl.Element
    rows = block * 32
    samples = pl.BlockSpec(
        (element(rows), element(PIECES), element(LANES)),
        lambda i, s: (pl.multiple_of(s[0] + i * rows, 16), 0, 0),
    )
    operands = [phase, weight, pool]
    in_specs = [samples, samples, pl.BlockSpec(pool.shape, lambda i, s: (0, 0))]
    aliases = {}
    if looked is not None:
        operands.append(looked)
        in_specs.append(pl.BlockSpec(memory_space=pl.ANY))
        aliases = {4: 1}
    operands.extend(after)
    in_specs.extend([pl.BlockSpec(memory_space=pl.ANY)] * len(after))
    return pl.pallas_call(
        look_kernel,
        grid_spec=pltpu.PrefetchScalarGridSpec(
            num_scalar_prefetch=1,
            grid=(count // block,),
            in_specs=in_specs,
            out_specs=[
                pl.BlockSpec((3, rows, LANES), lambda i, s: (0, i, 0)),
                pl.BlockSpec(
                    (element(GROUPS), element(block), element(8), element(LANES)),
                    lambda i, s: (0, slot + i * block, 0, 0),
                ),
            ],
            scratch_shapes=[pltpu.VMEM((GROUP * PITCH, LANES), jnp.float32)] * 2
            + [pltpu.VMEM((rows, RG_LOOKS * LANES), jnp.bfloat16)] * 8,
        ),
        out_shape=[
            jax.ShapeDtypeStruct((3, count * 32, LANES), jnp.float32),
            jax.ShapeDtypeStruct((GROUPS, slots, 8, LANES), jnp.float32),
        ],
        input_output_aliases=aliases,
        compiler_params=pltpu.CompilerParams(vmem_limit_bytes=56 * 1024 * 1024),
        cost_estimate=lasting(0.02),
        name="look_sums",
    )(start, *operands)


def window_kernel(near, own, mate, far, bands, *refs):
    own_out, mate_out, parts = refs[-3:]
    rows = own.shape[1]

    def divide(g, carry):
        r = pl.ds(pl.multiple_of(g * 32, 32), 32)
        for source, ref in enumerate((near, own, mate, far)):
            for quantity in range(3):
                value = ref[quantity, r, :]
                high = value.astype(jnp.bfloat16)
                low = (value - high.astype(jnp.float32)).astype(jnp.bfloat16)
                at = source * 2 * LANES
                parts[quantity, r, at : at + LANES] = high
                parts[quantity, r, at + LANES : at + 2 * LANES] = low
        return carry

    lax.fori_loop(0, rows // 32, divide, 0)
    lane = lax.broadcasted_iota(jnp.int32, (rows, LANES), 1)
    row = lax.rem(lax.broadcasted_iota(jnp.int32, (rows, LANES), 0), 32)
    upper = lane >= LANES // 2
    valid = (upper & (row < 31)) | (jnp.logical_not(upper) & (row > 0))
    for side, out in enumerate((own_out, mate_out)):
        sums = []
        for quantity in range(3):
            left = parts[quantity, :, side * 2 * LANES : (side + 3) * 2 * LANES]
            both = jnp.dot(left, bands[...], preferred_element_type=jnp.float32)
            edge = both[:, LANES:]
            edge = jnp.where(upper, pltpu.roll(edge, rows - 1, 0), pltpu.roll(edge, 1, 0))
            sums.append(both[:, :LANES] + jnp.where(valid, edge, 0.0))
        re, im, w = sums
        out[...] = jnp.sqrt(re * re + im * im) / w


def window_coherence(bands, near, own, mate, far, after=()):
    count = mate.shape[1]
    rows = count // 2
    part = pl.BlockSpec((3, rows, LANES), lambda i: (0, i, 0))
    out = pl.BlockSpec((rows, LANES), lambda i: (i, 0))
    return pl.pallas_call(
        window_kernel,
        grid=(2,),
        in_specs=[part] * 4
        + [pl.BlockSpec(bands.shape, lambda i: (0, 0))]
        + [pl.BlockSpec(memory_space=pl.ANY)] * len(after),
        out_specs=[out, out],
        out_shape=[jax.ShapeDtypeStruct((count, LANES), jnp.float32)] * 2,
        scratch_shapes=[pltpu.VMEM((3, rows, 8 * LANES), jnp.bfloat16)],
        compiler_params=pltpu.CompilerParams(vmem_limit_bytes=40 * 1024 * 1024),
        cost_estimate=lasting(0.02),
        name="window_coherence",
    )(near, own, mate, far, bands, *after)


def merge_kernel(odd, own_a, own_b, other_a, other_b, out):
    first, share = own_a.shape[0], own_a.shape[0] + own_b.shape[0]

    @pl.when(odd[0] == 0)
    def _():
        out[:first] = own_a[...]
        out[first:share] = own_b[...]
        out[share : share + first - 1] = other_a[1:]
        out[share + first - 1 :] = other_b[...]

    @pl.when(odd[0] != 0)
    def _():
        out[:first] = other_a[...]
        out[first:share] = other_b[...]
        out[share : share + first - 1] = own_a[1:]
        out[share + first - 1 :] = own_b[...]


def merge(odd, ifgs, *parts):
    vmem = pl.BlockSpec(memory_space=pltpu.VMEM)
    return pl.pallas_call(
        merge_kernel,
        in_specs=[pl.BlockSpec(memory_space=pltpu.SMEM)] + [vmem] * 4,
        out_specs=vmem,
        out_shape=jax.ShapeDtypeStruct((ifgs, *parts[0].shape[1:]), jnp.float32),
        compiler_params=pltpu.CompilerParams(vmem_limit_bytes=8 * 1024 * 1024),
        cost_estimate=lasting(0.3),
        name="merge",
    )(odd, *parts)


def unslot_kernel(where, *refs):
    parts, out = refs[:GROUPS], refs[-1]
    share = parts[0].shape[0] // 2
    rest = out.shape[0] - share
    odd = where[0]
    for d, part in enumerate(parts):
        chunk = pl.ds(jnp.bitwise_xor(where[1], d), 1)
        out[:share, chunk] = part[pl.ds(share * (1 - odd), share)][:, None]
        out[share:, chunk] = part[pl.ds(1 + share * odd, rest)][:, None]


def unslot(where, ifgs, parts, after):
    vmem = pl.BlockSpec(memory_space=pltpu.VMEM)
    return pl.pallas_call(
        unslot_kernel,
        in_specs=[pl.BlockSpec(memory_space=pltpu.SMEM)] + [vmem] * GROUPS
        + [pl.BlockSpec(memory_space=pl.ANY)] * len(after),
        out_specs=vmem,
        out_shape=jax.ShapeDtypeStruct((ifgs, GROUPS, *parts[0].shape[1:]), jnp.float32),
        compiler_params=pltpu.CompilerParams(vmem_limit_bytes=8 * 1024 * 1024),
        cost_estimate=lasting(50),
        name="unslot",
    )(where, *parts, *after)


def bands_kernel(row_off, col_off, flip, bands):
    gap = lax.broadcasted_iota(jnp.int32, (LANES, LANES), 1) - lax.broadcasted_iota(
        jnp.int32, (LANES, LANES), 0
    )
    for e in range(3):
        same = jnp.zeros((LANES, LANES), jnp.float32)
        next_to = jnp.zeros((LANES, LANES), jnp.float32)
        for k in range(OFFSETS):
            amount = jnp.where(row_off[k] * flip[0] == e - 1, 1.0, 0.0)
            moved = gap + col_off[k]
            same = same + jnp.where(moved == 0, amount, 0.0)
            next_to = next_to + jnp.where(jnp.abs(moved) == LANES, amount, 0.0)
        for half in range(2):
            rows = slice((2 * e + half) * LANES, (2 * e + half + 1) * LANES)
            bands[rows, :LANES] = same.astype(jnp.bfloat16)
            bands[rows, LANES:] = next_to.astype(jnp.bfloat16)


def window_bands(row_off, col_off, flip):
    return pl.pallas_call(
        bands_kernel,
        in_specs=[pl.BlockSpec(memory_space=pltpu.SMEM)] * 3,
        out_specs=pl.BlockSpec(memory_space=pltpu.VMEM),
        out_shape=jax.ShapeDtypeStruct((6 * LANES, 2 * LANES), jnp.bfloat16),
        cost_estimate=lasting(1),
        name="window_bands",
    )(row_off, col_off, flip)


def network_kernel(
    flip, dates, *refs, slots
):
    inverse, design, grid = refs[-3:]
    count = inverse.shape[0]
    date = lax.broadcasted_iota(jnp.int32, inverse.shape, 0) + 1
    signed = (dates[1:2] == date).astype(jnp.float32) - (dates[0:1] == date).astype(jnp.float32)
    design[...] = jnp.transpose(signed)
    slot = lax.rem(lax.broadcasted_iota(jnp.int32, inverse.shape, 1), slots)
    again = jnp.where(flip[0] > 0, 0, slots // 2 - 1)
    counted = jnp.where(slot == again, 0.0, signed)
    normal = lax.dot_general(
        counted.astype(jnp.bfloat16), signed.astype(jnp.bfloat16), (((1,), (1,)), ((), ())), preferred_element_type=jnp.float32
    )
    i = lax.broadcasted_iota(jnp.int32, (count, count), 0)
    j = lax.broadcasted_iota(jnp.int32, (count, count), 1)
    normal = normal + jnp.where(i == j, jnp.where(i == DATES - 1, 1.0, damping), 0.0)
    grid[0] = normal[:, :LANES]
    grid[1] = jnp.zeros((count, LANES), jnp.float32)
    grid[1, :, : count - LANES] = normal[:, LANES:]
    lane = lax.broadcasted_iota(jnp.int32, (1, LANES), 1)
    for first in range(0, count, 32):
        rows = min(first + 32 + REACH, count)
        tiles = range(1 if rows <= LANES else 2)
        half = first // LANES

        def sweep(k, carry):
            here = k - half * LANES
            picked = lane == here
            lines = [grid[t, pl.ds(k, 1), :] for t in tiles]
            values = [grid[t, :rows, :] for t in tiles]
            scale = 1.0 / jnp.sum(jnp.where(picked, lines[half], 0.0), axis=1, keepdims=True)
            lines = [line * scale for line in lines]
            lines[half] = jnp.where(picked, -scale, lines[half])
            index = jnp.full((rows, LANES), here, jnp.int32)
            column = jnp.take_along_axis(values[half], index, axis=1)
            values[half] = jnp.where(picked, 0.0, values[half])
            for t in tiles:
                grid[t, :rows, :] = values[t] - column * lines[t]
            for t in tiles:
                grid[t, pl.ds(k, 1), :] = lines[t]
            return carry

        lax.fori_loop(first, first + 32, sweep, 0)
    swept = jnp.concatenate([grid[0], grid[1, :, : count - LANES]], axis=1)
    inverse[...] = -jnp.dot(
        swept, counted, precision=lax.Precision.HIGHEST, preferred_element_type=jnp.float32
    )


def network_solve(flip, dates, slots, after=()):
    pairs = dates.shape[1]
    vmem = pl.BlockSpec(memory_space=pltpu.VMEM)
    smem = pl.BlockSpec(memory_space=pltpu.SMEM)
    return pl.pallas_call(
        functools.partial(network_kernel, slots=slots),
        in_specs=[smem, vmem] + [pl.BlockSpec(memory_space=pl.ANY)] * len(after),
        out_specs=[vmem] * 2,
        out_shape=[
            jax.ShapeDtypeStruct((DATES, pairs), jnp.float32),
            jax.ShapeDtypeStruct((pairs, DATES), jnp.float32),
        ],
        scratch_shapes=[pltpu.VMEM((2, DATES, LANES), jnp.float32)],
        compiler_params=pltpu.CompilerParams(vmem_limit_bytes=16 * 1024 * 1024),
        cost_estimate=lasting(0.02),
        name="network_solve",
    )(flip, dates, *after)


def invert_kernel(group, looked, inverse, design, *refs):
    *residuals, history, flat, held = refs[-GROUPS - 3 :]
    slots = residuals[0].shape[0]
    count = GROUPS * slots
    rows = looked.reshape(count * 8, LANES)
    for j in range(8):
        flat[:, j * LANES : (j + 1) * LANES] = rows[pl.ds(j, count, stride=8), :]
    phase = flat[...]

    def product(a, b):
        return jnp.dot(a, b, precision=lax.Precision.HIGHEST, preferred_element_type=jnp.float32)

    solved = product(inverse[...], phase)
    history[...] = jnp.transpose(solved)[:, : DATES - 1]
    rest = phase - product(design[...], solved)
    lines = held.reshape(count * 8, LANES)
    for j in range(8):
        lines[pl.ds(j, count, stride=8), :] = rest[:, j * LANES : (j + 1) * LANES]
    for d, residual in enumerate(residuals):
        residual[...] = held[pl.ds(jnp.bitwise_xor(group[0], d) * slots, slots)]


def invert(group, looked, inverse, design, after):
    slots = looked.shape[1]
    vmem = pl.BlockSpec(memory_space=pltpu.VMEM)
    part = jax.ShapeDtypeStruct((slots, 8, LANES), jnp.float32)
    return pl.pallas_call(
        invert_kernel,
        in_specs=[pl.BlockSpec(memory_space=pltpu.SMEM)]
        + [vmem] * 3
        + [pl.BlockSpec(memory_space=pl.ANY)] * len(after),
        out_specs=[vmem] * (GROUPS + 1),
        out_shape=[part] * GROUPS + [jax.ShapeDtypeStruct((8 * LANES, DATES - 1), jnp.float32)],
        scratch_shapes=[
            pltpu.VMEM((GROUPS * slots, 8 * LANES), jnp.float32),
            pltpu.VMEM((GROUPS * slots, 8, LANES), jnp.float32),
        ],
        compiler_params=pltpu.CompilerParams(vmem_limit_bytes=32 * 1024 * 1024),
        cost_estimate=lasting(0.02),
        name="invert",
    )(group, looked, inverse, design, *after)


def tiles(samples):
    ifgs, az, cols = samples.shape
    split = samples.reshape(ifgs, az, cols // LANES, LANES).transpose(0, 2, 1, 3)
    return split.reshape(ifgs * cols // (LANES * RG_LOOKS), PIECES, LANES)


def local(phase_samples, sample_weights, reference_date, secondary_date, window_rows, window_cols):
    ifgs = phase_samples.shape[0]
    row_count = lax.axis_size("rows")
    odd = lax.rem(lax.axis_index("rows"), 2)
    share = (ifgs + 1) // 2
    rest = ifgs - share
    mates = [(r, r ^ 1) for r in range(row_count)]
    outward = [(r, r + 2 if r % 2 else r - 2) for r in range(row_count)]
    outward = [(s, d) for s, d in outward if 0 <= d < row_count]
    across = [(r, r - 2 if r % 2 else r + 2) for r in range(row_count)]
    across = [(s, d) for s, d in across if 0 <= d < row_count]

    group = lax.axis_index("ifg")
    phase = tiles(phase_samples)
    weight = tiles(sample_weights)
    pool = pooling_matrix()
    flip = (1 - 2 * odd).reshape(1)
    side = odd.reshape(1)
    mine = rest * 32 * odd
    other = rest * 32 * (1 - odd)
    slots = 2 * share
    early = FIRST
    late = share - early

    sent_a, looked = look_sums(
        other.reshape(1), early, early // 2, 0, slots, phase, weight, pool
    )
    mate_a = lax.ppermute(sent_a, "rows", mates)
    sent_b, looked = look_sums(
        (other + early * 32).reshape(1), late, late // 2, early, slots, phase, weight, pool, looked
    )
    mate_b = lax.ppermute(sent_b, "rows", mates)
    own_a, looked = look_sums(
        mine.reshape(1), early, early // 2, share, slots, phase, weight, pool, looked
    )
    far_a = lax.ppermute(own_a, "rows", outward)
    own_b, looked = look_sums(
        (mine + early * 32).reshape(1), late, late // 2, share + early, slots,
        phase, weight, pool, looked, (mate_a,),
    )
    far_b = lax.ppermute(own_b, "rows", outward)
    near_a = lax.ppermute(mate_a, "rows", across)
    moved = lax.all_to_all(looked, "ifg", split_axis=0, concat_axis=0, tiled=True)

    dates = jnp.stack([reference_date, secondary_date]).reshape(2, GROUPS, ifgs)
    dates = jnp.where(
        odd == 0,
        jnp.concatenate([dates[:, :, rest:], dates[:, :, :share]], axis=2),
        jnp.concatenate([dates[:, :, :share], dates[:, :, rest:]], axis=2),
    ).reshape(2, -1)
    bands = window_bands(window_rows, window_cols, flip)
    near_b = lax.ppermute(mate_b, "rows", across)
    own_part_a, mate_part_a = window_coherence(
        bands, near_a, own_a, mate_a, far_a
    )
    back_a = lax.ppermute(mate_part_a, "rows", mates)
    inverse, design = network_solve(flip, dates, slots, (mate_b, mate_part_a))
    *residual, history = invert(
        group.reshape(1), moved, inverse, design, (back_a,)
    )
    residual = residual[:1] + [
        lax.ppermute(residual[d], "ifg", [(i, i ^ d) for i in range(GROUPS)])
        for d in range(1, GROUPS)
    ]
    own_part_b, mate_part_b = window_coherence(
        bands, near_b, own_b, mate_b, far_b, after=(residual[1], history)
    )
    back_b = lax.ppermute(mate_part_b, "rows", mates)

    by_ifg = (-1, 32, LANES)
    coherence = merge(
        side, ifgs, *[part.reshape(by_ifg) for part in (own_part_a, own_part_b, back_a, back_b)]
    )

    residual = unslot(jnp.stack([odd, group]), ifgs, residual, (coherence,))
    history = history.reshape(row_count, -1, DATES - 1)
    history = lax.all_to_all(history, "rows", split_axis=0, concat_axis=0, tiled=True)
    shape = (ifgs, 1, 32 * LANES)
    return (coherence.reshape(shape), residual.reshape(shape), history.transpose(2, 0, 1))


def solution(mesh):
    placed = (P("ifg", "rows", None), P("ifg", "rows", None), P(), P(), P(), P())
    return jax.shard_map(
        local,
        mesh=mesh,
        in_specs=placed,
        out_specs=(P("ifg", "rows", None), P("ifg", "rows", None), P(None, None, ("ifg", "rows"))),
        check_vma=False,
    )
```

```python
import functools
import math

import jax
import jax.numpy as jnp
import numpy as np
from jax import lax
from jax.experimental import pallas as pl
from jax.experimental.pallas import tpu as pltpu
from jax.sharding import PartitionSpec as P

DATES = 160
AZ_LOOKS = 2
RG_LOOKS = 8
REACH = 24
OFFSETS = 9
LANES = 128

damping = 0.25

SIN_QUARTER = (
    0.3535533845424652,
    -0.0036828448064625263,
    1.1508434909046628e-05,
    -1.7096880355893518e-08,
    1.4046378643550739e-11,
)
COS_QUARTER = (
    0.9999999403953552,
    -0.031249957159161568,
    0.00016275106463581324,
    -3.383578359716921e-07,
    3.553040917037009e-10,
)
SIN_SCALE = 2.0 * math.sqrt(2.0)

PIECES = 16
PITCH = 17
GROUPS = 4
FIRST = 20
GROUP = 16


def pooling_matrix():
    look = np.arange(LANES * RG_LOOKS) // RG_LOOKS
    return jnp.asarray(look[:, None] == np.arange(LANES), jnp.bfloat16)


def lasting(us):
    return pl.CostEstimate(flops=0, bytes_accessed=int(us * 3.6e6), transcendentals=0)


def horner(coefficients, z):
    total = coefficients[-1] * z + coefficients[-2]
    for c in coefficients[-3::-1]:
        total = total * z + c
    return total


def regroup(ref, held, rows):
    tiles = ref[rows].astype(jnp.float32)
    for m in range(GROUP):
        held[m * PITCH : m * PITCH + PIECES, :] = tiles[m]


def piece(held, q):
    return held[pl.ds(q, GROUP, stride=PITCH), :]


def split_store(high, low, rows, c, value):
    top = value.astype(jnp.bfloat16)
    high[rows, c * LANES : (c + 1) * LANES] = top
    low[rows, c * LANES : (c + 1) * LANES] = (value - top.astype(jnp.float32)).astype(jnp.bfloat16)


def pooled(high, low, pool):
    return jnp.dot(high[...], pool[...], preferred_element_type=jnp.float32) + jnp.dot(
        low[...], pool[...], preferred_element_type=jnp.float32
    )


def look_kernel(start, phase, weight, pool, *refs):
    out, looked, p_held, w_held, wh, wl, ph, plo, sh, sl, qh, ql = refs[-12:]
    block = phase.shape[0]

    def step(g, carry):
        rows = pl.ds(pl.multiple_of(g * GROUP, GROUP), GROUP)
        regroup(phase, p_held, rows)
        regroup(weight, w_held, rows)
        for c in range(RG_LOOKS):
            sums = None
            for a in range(AZ_LOOKS):
                x = piece(p_held, 2 * c + a)
                w = piece(w_held, 2 * c + a)
                z = x * x
                s = x * horner(SIN_QUARTER, z)
                k = horner(COS_QUARTER, z)
                half = s * k
                terms = (w, w * x, w * (half * (1.0 - s * s)), w * (half * half))
                sums = terms if sums is None else [t + u for t, u in zip(sums, terms)]
            for value, high, low in zip(sums, (wh, ph, sh, qh), (wl, plo, sl, ql)):
                split_store(high, low, rows, c, value)
        return carry

    lax.fori_loop(0, block // GROUP, step, 0)
    total = pooled(wh, wl, pool)
    mean = pooled(ph, plo, pool) / total
    looked[...] = jnp.transpose(mean.reshape(block // 32, GROUPS, 8, LANES), (1, 0, 2, 3))
    out[0] = total - 4.0 * pooled(qh, ql, pool)
    out[1] = SIN_SCALE * pooled(sh, sl, pool)
    out[2] = total


def look_sums(start, count, block, slot, slots, phase, weight, pool, looked=None, after=()):
    element = pl.Element
    rows = block * 32
    samples = pl.BlockSpec(
        (element(rows), element(PIECES), element(LANES)),
        lambda i, s: (pl.multiple_of(s[0] + i * rows, 16), 0, 0),
    )
    operands = [phase, weight, pool]
    in_specs = [samples, samples, pl.BlockSpec(pool.shape, lambda i, s: (0, 0))]
    aliases = {}
    if looked is not None:
        operands.append(looked)
        in_specs.append(pl.BlockSpec(memory_space=pl.ANY))
        aliases = {4: 1}
    operands.extend(after)
    in_specs.extend([pl.BlockSpec(memory_space=pl.ANY)] * len(after))
    return pl.pallas_call(
        look_kernel,
        grid_spec=pltpu.PrefetchScalarGridSpec(
            num_scalar_prefetch=1,
            grid=(count // block,),
            in_specs=in_specs,
            out_specs=[
                pl.BlockSpec((3, rows, LANES), lambda i, s: (0, i, 0)),
                pl.BlockSpec(
                    (element(GROUPS), element(block), element(8), element(LANES)),
                    lambda i, s: (0, slot + i * block, 0, 0),
                ),
            ],
            scratch_shapes=[pltpu.VMEM((GROUP * PITCH, LANES), jnp.float32)] * 2
            + [pltpu.VMEM((rows, RG_LOOKS * LANES), jnp.bfloat16)] * 8,
        ),
        out_shape=[
            jax.ShapeDtypeStruct((3, count * 32, LANES), jnp.float32),
            jax.ShapeDtypeStruct((GROUPS, slots, 8, LANES), jnp.float32),
        ],
        input_output_aliases=aliases,
        compiler_params=pltpu.CompilerParams(vmem_limit_bytes=56 * 1024 * 1024),
        cost_estimate=lasting(0.02),
        name="look_sums",
    )(start, *operands)


def window_kernel(row_off, col_off, flip, near, own, mate, far, *refs):
    own_out, mate_out, parts, bands = refs[-4:]
    rows = own.shape[1]

    @pl.when(pl.program_id(0) == 0)
    def _():
        window_bands(row_off, col_off, flip, bands)

    def divide(g, carry):
        r = pl.ds(pl.multiple_of(g * 32, 32), 32)
        for source, ref in enumerate((near, own, mate, far)):
            for quantity in range(3):
                value = ref[quantity, r, :]
                high = value.astype(jnp.bfloat16)
                low = (value - high.astype(jnp.float32)).astype(jnp.bfloat16)
                at = source * 2 * LANES
                parts[quantity, r, at : at + LANES] = high
                parts[quantity, r, at + LANES : at + 2 * LANES] = low
        return carry

    lax.fori_loop(0, rows // 32, divide, 0)
    lane = lax.broadcasted_iota(jnp.int32, (rows, LANES), 1)
    row = lax.rem(lax.broadcasted_iota(jnp.int32, (rows, LANES), 0), 32)
    upper = lane >= LANES // 2
    valid = (upper & (row < 31)) | (jnp.logical_not(upper) & (row > 0))
    for side, out in enumerate((own_out, mate_out)):
        sums = []
        for quantity in range(3):
            left = parts[quantity, :, side * 2 * LANES : (side + 3) * 2 * LANES]
            both = jnp.dot(left, bands[...], preferred_element_type=jnp.float32)
            edge = both[:, LANES:]
            edge = jnp.where(upper, pltpu.roll(edge, rows - 1, 0), pltpu.roll(edge, 1, 0))
            sums.append(both[:, :LANES] + jnp.where(valid, edge, 0.0))
        re, im, w = sums
        out[...] = jnp.sqrt(re * re + im * im) / w


def window_coherence(offsets, near, own, mate, far, after=()):
    count = mate.shape[1]
    rows = count // 2
    part = pl.BlockSpec((3, rows, LANES), lambda i: (0, i, 0))
    out = pl.BlockSpec((rows, LANES), lambda i: (i, 0))
    return pl.pallas_call(
        window_kernel,
        grid=(2,),
        in_specs=[pl.BlockSpec(memory_space=pltpu.SMEM)] * 3
        + [part] * 4
        + [pl.BlockSpec(memory_space=pl.ANY)] * len(after),
        out_specs=[out, out],
        out_shape=[jax.ShapeDtypeStruct((count, LANES), jnp.float32)] * 2,
        scratch_shapes=[
            pltpu.VMEM((3, rows, 8 * LANES), jnp.bfloat16),
            pltpu.VMEM((6 * LANES, 2 * LANES), jnp.bfloat16),
        ],
        compiler_params=pltpu.CompilerParams(vmem_limit_bytes=40 * 1024 * 1024),
        cost_estimate=lasting(0.02),
        name="window_coherence",
    )(*offsets, near, own, mate, far, *after)


def merge_kernel(odd, own_a, own_b, other_a, other_b, *refs):
    out = refs[-1]
    first, share = own_a.shape[0], own_a.shape[0] + own_b.shape[0]

    @pl.when(odd[0] == 0)
    def _():
        out[:first] = own_a[...]
        out[first:share] = own_b[...]
        out[share : share + first - 1] = other_a[1:]
        out[share + first - 1 :] = other_b[...]

    @pl.when(odd[0] != 0)
    def _():
        out[:first] = other_a[...]
        out[first:share] = other_b[...]
        out[share : share + first - 1] = own_a[1:]
        out[share + first - 1 :] = own_b[...]


def merge(odd, ifgs, *parts, after):
    vmem = pl.BlockSpec(memory_space=pltpu.VMEM)
    return pl.pallas_call(
        merge_kernel,
        in_specs=[pl.BlockSpec(memory_space=pltpu.SMEM)] + [vmem] * 4
        + [pl.BlockSpec(memory_space=pl.ANY)] * len(after),
        out_specs=vmem,
        out_shape=jax.ShapeDtypeStruct((ifgs, *parts[0].shape[1:]), jnp.float32),
        compiler_params=pltpu.CompilerParams(vmem_limit_bytes=8 * 1024 * 1024),
        cost_estimate=lasting(0.3),
        name="merge",
    )(odd, *parts, *after)


def unslot_kernel(where, *refs):
    parts, out = refs[:GROUPS], refs[-1]
    share = parts[0].shape[0] // 2
    rest = out.shape[0] - share
    odd = where[0]
    for d, part in enumerate(parts):
        chunk = pl.ds(jnp.bitwise_xor(where[1], d), 1)
        out[:share, chunk] = part[pl.ds(share * (1 - odd), share)][:, None]
        out[share:, chunk] = part[pl.ds(1 + share * odd, rest)][:, None]


def unslot(where, ifgs, parts, after):
    vmem = pl.BlockSpec(memory_space=pltpu.VMEM)
    return pl.pallas_call(
        unslot_kernel,
        in_specs=[pl.BlockSpec(memory_space=pltpu.SMEM)] + [vmem] * GROUPS
        + [pl.BlockSpec(memory_space=pl.ANY)] * len(after),
        out_specs=vmem,
        out_shape=jax.ShapeDtypeStruct((ifgs, GROUPS, *parts[0].shape[1:]), jnp.float32),
        compiler_params=pltpu.CompilerParams(vmem_limit_bytes=8 * 1024 * 1024),
        cost_estimate=lasting(50),
        name="unslot",
    )(where, *parts, *after)


def window_bands(row_off, col_off, flip, bands):
    gap = lax.broadcasted_iota(jnp.int32, (LANES, LANES), 1) - lax.broadcasted_iota(
        jnp.int32, (LANES, LANES), 0
    )
    for e in range(3):
        same = jnp.zeros((LANES, LANES), jnp.float32)
        next_to = jnp.zeros((LANES, LANES), jnp.float32)
        for k in range(OFFSETS):
            amount = jnp.where(row_off[k] * flip[0] == e - 1, 1.0, 0.0)
            moved = gap + col_off[k]
            same = same + jnp.where(moved == 0, amount, 0.0)
            next_to = next_to + jnp.where(jnp.abs(moved) == LANES, amount, 0.0)
        for half in range(2):
            rows = slice((2 * e + half) * LANES, (2 * e + half + 1) * LANES)
            bands[rows, :LANES] = same.astype(jnp.bfloat16)
            bands[rows, LANES:] = next_to.astype(jnp.bfloat16)


def network_kernel(
    flip, dates, *refs, slots
):
    inverse, design, grid = refs[-3:]
    count = inverse.shape[0]
    date = lax.broadcasted_iota(jnp.int32, inverse.shape, 0) + 1
    signed = (dates[1:2] == date).astype(jnp.float32) - (dates[0:1] == date).astype(jnp.float32)
    design[...] = jnp.transpose(signed)
    slot = lax.rem(lax.broadcasted_iota(jnp.int32, inverse.shape, 1), slots)
    again = jnp.where(flip[0] > 0, 0, slots // 2 - 1)
    counted = jnp.where(slot == again, 0.0, signed)
    normal = lax.dot_general(
        counted.astype(jnp.bfloat16), signed.astype(jnp.bfloat16), (((1,), (1,)), ((), ())), preferred_element_type=jnp.float32
    )
    i = lax.broadcasted_iota(jnp.int32, (count, count), 0)
    j = lax.broadcasted_iota(jnp.int32, (count, count), 1)
    normal = normal + jnp.where(i == j, jnp.where(i == DATES - 1, 1.0, damping), 0.0)
    grid[0] = normal[:, :LANES]
    grid[1] = jnp.zeros((count, LANES), jnp.float32)
    grid[1, :, : count - LANES] = normal[:, LANES:]
    lane = lax.broadcasted_iota(jnp.int32, (1, LANES), 1)
    for first in range(0, count, 32):
        rows = min(first + 32 + REACH, count)
        tiles = range(1 if rows <= LANES else 2)
        half = first // LANES

        def sweep(k, carry):
            here = k - half * LANES
            picked = lane == here
            lines = [grid[t, pl.ds(k, 1), :] for t in tiles]
            values = [grid[t, :rows, :] for t in tiles]
            index = jnp.full((rows, LANES), here, jnp.int32)
            column = jnp.take_along_axis(values[half], index, axis=1)
            scale = 1.0 / jnp.take_along_axis(jnp.broadcast_to(lines[half], (8, LANES)), index[:8], axis=1)[:1]
            lines = [line * scale for line in lines]
            lines[half] = jnp.where(picked, -scale, lines[half])
            values[half] = jnp.where(picked, 0.0, values[half])
            for t in tiles:
                grid[t, :rows, :] = values[t] - column * lines[t]
            for t in tiles:
                grid[t, pl.ds(k, 1), :] = lines[t]
            return carry

        lax.fori_loop(first, first + 32, sweep, 0)
    swept = jnp.concatenate([grid[0], grid[1, :, : count - LANES]], axis=1)
    inverse[...] = -jnp.dot(
        swept, counted, precision=lax.Precision.HIGHEST, preferred_element_type=jnp.float32
    )


def network_solve(flip, dates, slots, after=()):
    pairs = dates.shape[1]
    vmem = pl.BlockSpec(memory_space=pltpu.VMEM)
    smem = pl.BlockSpec(memory_space=pltpu.SMEM)
    return pl.pallas_call(
        functools.partial(network_kernel, slots=slots),
        in_specs=[smem, vmem] + [pl.BlockSpec(memory_space=pl.ANY)] * len(after),
        out_specs=[vmem] * 2,
        out_shape=[
            jax.ShapeDtypeStruct((DATES, pairs), jnp.float32),
            jax.ShapeDtypeStruct((pairs, DATES), jnp.float32),
        ],
        scratch_shapes=[pltpu.VMEM((2, DATES, LANES), jnp.float32)],
        compiler_params=pltpu.CompilerParams(vmem_limit_bytes=16 * 1024 * 1024),
        cost_estimate=lasting(0.02),
        name="network_solve",
    )(flip, dates, *after)


def invert_kernel(group, looked, inverse, design, *refs):
    *residuals, history, flat, held = refs[-GROUPS - 3 :]
    slots = residuals[0].shape[0]
    count = GROUPS * slots
    rows = looked.reshape(count * 8, LANES)
    for j in range(8):
        flat[:, j * LANES : (j + 1) * LANES] = rows[pl.ds(j, count, stride=8), :]
    phase = flat[...]

    def product(a, b):
        return jnp.dot(a, b, precision=lax.Precision.HIGHEST, preferred_element_type=jnp.float32)

    solved = product(inverse[...], phase)
    blocks = history.shape[0]
    history[:, :32] = jnp.transpose(solved[:LANES]).reshape(blocks, 32, LANES)
    last = DATES - LANES
    rest = jnp.concatenate([solved[LANES:], jnp.zeros((LANES - last, 8 * LANES), jnp.float32)])
    rest = jnp.transpose(rest).reshape(blocks, 4, 8, LANES)
    packed = rest[:, 0]
    for b in range(1, 4):
        packed = packed + pltpu.roll(rest[:, b], b * last, 2)
    history[:, 32:] = packed
    rest = phase - product(design[...], solved)
    lines = held.reshape(count * 8, LANES)
    for j in range(8):
        lines[pl.ds(j, count, stride=8), :] = rest[:, j * LANES : (j + 1) * LANES]
    for d, residual in enumerate(residuals):
        residual[...] = held[pl.ds(jnp.bitwise_xor(group[0], d) * slots, slots)]


def invert(group, looked, inverse, design, after):
    slots = looked.shape[1]
    vmem = pl.BlockSpec(memory_space=pltpu.VMEM)
    part = jax.ShapeDtypeStruct((slots, 8, LANES), jnp.float32)
    return pl.pallas_call(
        invert_kernel,
        in_specs=[pl.BlockSpec(memory_space=pltpu.SMEM)]
        + [vmem] * 3
        + [pl.BlockSpec(memory_space=pl.ANY)] * len(after),
        out_specs=[vmem] * (GROUPS + 1),
        out_shape=[part] * GROUPS + [jax.ShapeDtypeStruct((8 * LANES // 32, 40, LANES), jnp.float32)],
        scratch_shapes=[
            pltpu.VMEM((GROUPS * slots, 8 * LANES), jnp.float32),
            pltpu.VMEM((GROUPS * slots, 8, LANES), jnp.float32),
        ],
        compiler_params=pltpu.CompilerParams(vmem_limit_bytes=32 * 1024 * 1024),
        cost_estimate=lasting(0.02),
        name="invert",
    )(group, looked, inverse, design, *after)


def unpack_kernel(held, out):
    last = DATES - LANES
    out[:, :, :LANES] = held[:, :32]
    packed = held[:, 32:]
    for b in range(4):
        value = packed if b == 0 else pltpu.roll(packed, LANES - b * last, 2)
        out[:, 8 * b : 8 * (b + 1), LANES:] = value[:, :, : last - 1]


def unpack(held):
    vmem = pl.BlockSpec(memory_space=pltpu.VMEM)
    return pl.pallas_call(
        unpack_kernel,
        in_specs=[vmem],
        out_specs=vmem,
        out_shape=jax.ShapeDtypeStruct((held.shape[0], 32, DATES - 1), jnp.float32),
        compiler_params=pltpu.CompilerParams(vmem_limit_bytes=8 * 1024 * 1024),
        cost_estimate=lasting(0.3),
        name="unpack",
    )(held)


def tiles(samples):
    ifgs, az, cols = samples.shape
    split = samples.reshape(ifgs, az, cols // LANES, LANES).transpose(0, 2, 1, 3)
    return split.reshape(ifgs * cols // (LANES * RG_LOOKS), PIECES, LANES)


def local(phase_samples, sample_weights, reference_date, secondary_date, window_rows, window_cols):
    ifgs = phase_samples.shape[0]
    row_count = lax.axis_size("rows")
    odd = lax.rem(lax.axis_index("rows"), 2)
    share = (ifgs + 1) // 2
    rest = ifgs - share
    mates = [(r, r ^ 1) for r in range(row_count)]
    outward = [(r, r + 2 if r % 2 else r - 2) for r in range(row_count)]
    outward = [(s, d) for s, d in outward if 0 <= d < row_count]
    across = [(r, r - 2 if r % 2 else r + 2) for r in range(row_count)]
    across = [(s, d) for s, d in across if 0 <= d < row_count]

    group = lax.axis_index("ifg")
    phase = tiles(phase_samples)
    weight = tiles(sample_weights)
    pool = pooling_matrix()
    flip = (1 - 2 * odd).reshape(1)
    side = odd.reshape(1)
    mine = rest * 32 * odd
    other = rest * 32 * (1 - odd)
    slots = 2 * share
    early = FIRST
    late = share - early

    sent_a, looked = look_sums(
        other.reshape(1), early, early // 2, 0, slots, phase, weight, pool
    )
    mate_a = lax.ppermute(sent_a, "rows", mates)
    sent_b, looked = look_sums(
        (other + early * 32).reshape(1), late, late // 2, early, slots, phase, weight, pool, looked
    )
    mate_b = lax.ppermute(sent_b, "rows", mates)
    own_a, looked = look_sums(
        mine.reshape(1), early, early // 2, share, slots, phase, weight, pool, looked
    )
    far_a = lax.ppermute(own_a, "rows", outward)
    own_b, looked = look_sums(
        (mine + early * 32).reshape(1), late, late // 2, share + early, slots,
        phase, weight, pool, looked, (mate_a,),
    )
    far_b = lax.ppermute(own_b, "rows", outward)
    near_a = lax.ppermute(mate_a, "rows", across)
    moved = lax.all_to_all(looked, "ifg", split_axis=0, concat_axis=0, tiled=True)

    dates = jnp.stack([reference_date, secondary_date]).reshape(2, GROUPS, ifgs)
    dates = jnp.where(
        odd == 0,
        jnp.concatenate([dates[:, :, rest:], dates[:, :, :share]], axis=2),
        jnp.concatenate([dates[:, :, :share], dates[:, :, rest:]], axis=2),
    ).reshape(2, -1)
    offsets = (window_rows, window_cols, flip)
    near_b = lax.ppermute(mate_b, "rows", across)
    own_part_a, mate_part_a = window_coherence(
        offsets, near_a, own_a, mate_a, far_a
    )
    back_a = lax.ppermute(mate_part_a, "rows", mates)
    inverse, design = network_solve(flip, dates, slots, (mate_b, mate_part_a))
    *residual, history = invert(
        group.reshape(1), moved, inverse, design, (back_a,)
    )
    residual = residual[:1] + [
        lax.ppermute(residual[d], "ifg", [(i, i ^ d) for i in range(GROUPS)])
        for d in range(1, GROUPS)
    ]
    own_part_b, mate_part_b = window_coherence(
        offsets, near_b, own_b, mate_b, far_b, after=(residual[1], history)
    )
    back_b = lax.ppermute(mate_part_b, "rows", mates)

    residual = unslot(jnp.stack([odd, group]), ifgs, residual, ())
    by_ifg = (-1, 32, LANES)
    coherence = merge(
        side, ifgs, *[part.reshape(by_ifg) for part in (own_part_a, own_part_b, back_a, back_b)],
        after=(residual,),
    )

    history = lax.all_to_all(history, "rows", split_axis=0, concat_axis=0, tiled=True)
    shape = (ifgs, 1, 32 * LANES)
    return (coherence.reshape(shape), residual.reshape(shape), unpack(history).transpose(2, 0, 1))


def solution(mesh):
    placed = (P("ifg", "rows", None), P("ifg", "rows", None), P(), P(), P(), P())
    return jax.shard_map(
        local,
        mesh=mesh,
        in_specs=placed,
        out_specs=(P("ifg", "rows", None), P("ifg", "rows", None), P(None, None, ("ifg", "rows"))),
        check_vma=False,
    )
```

```python
import functools
import math

import jax
import jax.numpy as jnp
import numpy as np
from jax import lax
from jax.experimental import pallas as pl
from jax.experimental.pallas import tpu as pltpu
from jax.sharding import PartitionSpec as P

DATES = 160
AZ_LOOKS = 2
RG_LOOKS = 8
REACH = 24
OFFSETS = 9
LANES = 128

damping = 0.25

SIN_QUARTER = (
    0.3535533845424652,
    -0.0036828448064625263,
    1.1508434909046628e-05,
    -1.7096880355893518e-08,
    1.4046378643550739e-11,
)
COS_QUARTER = (
    0.9999999403953552,
    -0.031249957159161568,
    0.00016275106463581324,
    -3.383578359716921e-07,
    3.553040917037009e-10,
)
SIN_SCALE = 2.0 * math.sqrt(2.0)

PIECES = 16
PITCH = 17
VMEM_BYTES = 60 * 1024 * 1024
GROUPS = 4
FIRST = 20
GROUP = 16


def pooling_matrix():
    look = np.arange(LANES * RG_LOOKS) // RG_LOOKS
    return jnp.asarray(look[:, None] == np.arange(LANES), jnp.bfloat16)


def lasting(us):
    return pl.CostEstimate(flops=0, bytes_accessed=int(us * 3.6e6), transcendentals=0)


def whole(x):
    zeros = (0,) * len(x.shape)
    return pl.BlockSpec(x.shape, lambda i: zeros)


def horner(coefficients, z):
    total = coefficients[-1] * z + coefficients[-2]
    for c in coefficients[-3::-1]:
        total = total * z + c
    return total


def regroup(ref, held, rows):
    tiles = ref[rows].astype(jnp.float32)
    for m in range(GROUP):
        held[m * PITCH : m * PITCH + PIECES, :] = tiles[m]


def piece(held, q):
    return held[pl.ds(q, GROUP, stride=PITCH), :]


def split_store(high, low, rows, c, value):
    top = value.astype(jnp.bfloat16)
    high[rows, c * LANES : (c + 1) * LANES] = top
    low[rows, c * LANES : (c + 1) * LANES] = (value - top.astype(jnp.float32)).astype(jnp.bfloat16)


def pooled(high, low, pool):
    return jnp.dot(high[...], pool[...], preferred_element_type=jnp.float32) + jnp.dot(
        low[...], pool[...], preferred_element_type=jnp.float32
    )


def look_kernel(start, phase, weight, pool, *refs):
    out, looked, p_held, w_held, wh, wl, ph, plo, sh, sl, qh, ql = refs[-12:]
    block = phase.shape[0]

    def step(g, carry):
        rows = pl.ds(pl.multiple_of(g * GROUP, GROUP), GROUP)
        regroup(phase, p_held, rows)
        regroup(weight, w_held, rows)
        for c in range(RG_LOOKS):
            sums = None
            for a in range(AZ_LOOKS):
                x = piece(p_held, 2 * c + a)
                w = piece(w_held, 2 * c + a)
                z = x * x
                s = x * horner(SIN_QUARTER, z)
                k = horner(COS_QUARTER, z)
                half = s * k
                terms = (w, w * x, w * (half * (1.0 - s * s)), w * (half * half))
                sums = terms if sums is None else [t + u for t, u in zip(sums, terms)]
            for value, high, low in zip(sums, (wh, ph, sh, qh), (wl, plo, sl, ql)):
                split_store(high, low, rows, c, value)
        return carry

    lax.fori_loop(0, block // GROUP, step, 0)
    total = pooled(wh, wl, pool)
    mean = pooled(ph, plo, pool) / total
    looked[...] = jnp.transpose(mean.reshape(block // 32, GROUPS, 8, LANES), (1, 0, 2, 3))
    out[0] = total - 4.0 * pooled(qh, ql, pool)
    out[1] = SIN_SCALE * pooled(sh, sl, pool)
    out[2] = total


def look_sums(start, count, block, slot, slots, phase, weight, pool, looked=None, after=()):
    element = pl.Element
    rows = block * 32
    samples = pl.BlockSpec(
        (element(rows), element(PIECES), element(LANES)),
        lambda i, s: (pl.multiple_of(s[0] + i * rows, 16), 0, 0),
    )
    operands = [phase, weight, pool]
    in_specs = [samples, samples, pl.BlockSpec(pool.shape, lambda i, s: (0, 0))]
    aliases = {}
    if looked is not None:
        operands.append(looked)
        in_specs.append(pl.BlockSpec(memory_space=pl.ANY))
        aliases = {4: 1}
    operands.extend(after)
    in_specs.extend([pl.BlockSpec(memory_space=pl.ANY)] * len(after))
    return pl.pallas_call(
        look_kernel,
        grid_spec=pltpu.PrefetchScalarGridSpec(
            num_scalar_prefetch=1,
            grid=(count // block,),
            in_specs=in_specs,
            out_specs=[
                pl.BlockSpec((3, rows, LANES), lambda i, s: (0, i, 0)),
                pl.BlockSpec(
                    (element(GROUPS), element(block), element(8), element(LANES)),
                    lambda i, s: (0, slot + i * block, 0, 0),
                ),
            ],
            scratch_shapes=[pltpu.VMEM((GROUP * PITCH, LANES), jnp.float32)] * 2
            + [pltpu.VMEM((rows, RG_LOOKS * LANES), jnp.bfloat16)] * 8,
        ),
        out_shape=[
            jax.ShapeDtypeStruct((3, count * 32, LANES), jnp.float32),
            jax.ShapeDtypeStruct((GROUPS, slots, 8, LANES), jnp.float32),
        ],
        input_output_aliases=aliases,
        compiler_params=pltpu.CompilerParams(vmem_limit_bytes=56 * 1024 * 1024),
        cost_estimate=lasting(0.02),
        name="look_sums",
    )(start, *operands)


def window_kernel(row_off, col_off, flip, near, own, mate, far, *refs):
    own_out, mate_out, parts, bands = refs[-4:]
    rows = own.shape[1]

    @pl.when(pl.program_id(0) == 0)
    def _():
        window_bands(row_off, col_off, flip, bands)

    def divide(g, carry):
        r = pl.ds(pl.multiple_of(g * 32, 32), 32)
        for source, ref in enumerate((near, own, mate, far)):
            for quantity in range(3):
                value = ref[quantity, r, :]
                high = value.astype(jnp.bfloat16)
                low = (value - high.astype(jnp.float32)).astype(jnp.bfloat16)
                at = source * 2 * LANES
                parts[quantity, r, at : at + LANES] = high
                parts[quantity, r, at + LANES : at + 2 * LANES] = low
        return carry

    lax.fori_loop(0, rows // 32, divide, 0)
    lane = lax.broadcasted_iota(jnp.int32, (rows, LANES), 1)
    row = lax.rem(lax.broadcasted_iota(jnp.int32, (rows, LANES), 0), 32)
    upper = lane >= LANES // 2
    valid = (upper & (row < 31)) | (jnp.logical_not(upper) & (row > 0))
    for side, out in enumerate((own_out, mate_out)):
        sums = []
        for quantity in range(3):
            left = parts[quantity, :, side * 2 * LANES : (side + 3) * 2 * LANES]
            both = jnp.dot(left, bands[...], preferred_element_type=jnp.float32)
            edge = both[:, LANES:]
            edge = jnp.where(upper, pltpu.roll(edge, rows - 1, 0), pltpu.roll(edge, 1, 0))
            sums.append(both[:, :LANES] + jnp.where(valid, edge, 0.0))
        re, im, w = sums
        out[...] = jnp.sqrt(re * re + im * im) / w


def window_coherence(offsets, near, own, mate, far, after=()):
    count = mate.shape[1]
    rows = count // 2
    part = pl.BlockSpec((3, rows, LANES), lambda i: (0, i, 0))
    out = pl.BlockSpec((rows, LANES), lambda i: (i, 0))
    return pl.pallas_call(
        window_kernel,
        grid=(2,),
        in_specs=[pl.BlockSpec(memory_space=pltpu.SMEM)] * 3
        + [part] * 4
        + [pl.BlockSpec(memory_space=pl.ANY)] * len(after),
        out_specs=[out, out],
        out_shape=[jax.ShapeDtypeStruct((count, LANES), jnp.float32)] * 2,
        scratch_shapes=[
            pltpu.VMEM((3, rows, 8 * LANES), jnp.bfloat16),
            pltpu.VMEM((6 * LANES, 2 * LANES), jnp.bfloat16),
        ],
        compiler_params=pltpu.CompilerParams(vmem_limit_bytes=24 * 1024 * 1024),
        cost_estimate=lasting(0.02),
        name="window_coherence",
    )(*offsets, near, own, mate, far, *after)


def merge_kernel(odd, own_a, own_b, other_a, other_b, *refs):
    out = refs[-1]
    first, share = own_a.shape[0], own_a.shape[0] + own_b.shape[0]

    @pl.when(odd[0] == 0)
    def _():
        out[:first] = own_a[...]
        out[first:share] = own_b[...]
        out[share : share + first - 1] = other_a[1:]
        out[share + first - 1 :] = other_b[...]

    @pl.when(odd[0] != 0)
    def _():
        out[:first] = other_a[...]
        out[first:share] = other_b[...]
        out[share : share + first - 1] = own_a[1:]
        out[share + first - 1 :] = own_b[...]


def merge(odd, ifgs, *parts, after):
    output = jax.ShapeDtypeStruct((ifgs, *parts[0].shape[1:]), jnp.float32)
    return pl.pallas_call(
        merge_kernel,
        grid=(1,),
        in_specs=[pl.BlockSpec(memory_space=pltpu.SMEM)]
        + [whole(x) for x in parts]
        + [pl.BlockSpec(memory_space=pl.ANY)] * len(after),
        out_specs=whole(output),
        out_shape=output,
        compiler_params=pltpu.CompilerParams(vmem_limit_bytes=24 * 1024 * 1024),
        cost_estimate=lasting(0.3),
        name="merge",
    )(odd, *parts, *after)


def unslot_kernel(where, *refs):
    parts, out = refs[:GROUPS], refs[-1]
    share = parts[0].shape[0] // 2
    rest = out.shape[0] - share
    odd = where[0]
    for d, part in enumerate(parts):
        chunk = pl.ds(jnp.bitwise_xor(where[1], d), 1)
        out[:share, chunk] = part[pl.ds(share * (1 - odd), share)][:, None]
        out[share:, chunk] = part[pl.ds(1 + share * odd, rest)][:, None]


def unslot(where, ifgs, parts, after):
    output = jax.ShapeDtypeStruct((ifgs, GROUPS, *parts[0].shape[1:]), jnp.float32)
    return pl.pallas_call(
        unslot_kernel,
        grid=(1,),
        in_specs=[pl.BlockSpec(memory_space=pltpu.SMEM)]
        + [whole(x) for x in parts]
        + [pl.BlockSpec(memory_space=pl.ANY)] * len(after),
        out_specs=whole(output),
        out_shape=output,
        compiler_params=pltpu.CompilerParams(vmem_limit_bytes=24 * 1024 * 1024),
        cost_estimate=lasting(50),
        name="unslot",
    )(where, *parts, *after)


def window_bands(row_off, col_off, flip, bands):
    gap = lax.broadcasted_iota(jnp.int32, (LANES, LANES), 1) - lax.broadcasted_iota(
        jnp.int32, (LANES, LANES), 0
    )
    for e in range(3):
        same = jnp.zeros((LANES, LANES), jnp.float32)
        next_to = jnp.zeros((LANES, LANES), jnp.float32)
        for k in range(OFFSETS):
            amount = jnp.where(row_off[k] * flip[0] == e - 1, 1.0, 0.0)
            moved = gap + col_off[k]
            same = same + jnp.where(moved == 0, amount, 0.0)
            next_to = next_to + jnp.where(jnp.abs(moved) == LANES, amount, 0.0)
        for half in range(2):
            rows = slice((2 * e + half) * LANES, (2 * e + half + 1) * LANES)
            bands[rows, :LANES] = same.astype(jnp.bfloat16)
            bands[rows, LANES:] = next_to.astype(jnp.bfloat16)


def network_kernel(
    flip, dates, *refs, slots
):
    inverse, design, grid = refs[-3:]
    count = inverse.shape[0]
    date = lax.broadcasted_iota(jnp.int32, inverse.shape, 0) + 1
    signed = (dates[1:2] == date).astype(jnp.float32) - (dates[0:1] == date).astype(jnp.float32)
    design[...] = jnp.transpose(signed)
    slot = lax.rem(lax.broadcasted_iota(jnp.int32, inverse.shape, 1), slots)
    again = jnp.where(flip[0] > 0, 0, slots // 2 - 1)
    counted = jnp.where(slot == again, 0.0, signed)
    normal = lax.dot_general(
        counted.astype(jnp.bfloat16), signed.astype(jnp.bfloat16), (((1,), (1,)), ((), ())), preferred_element_type=jnp.float32
    )
    i = lax.broadcasted_iota(jnp.int32, (count, count), 0)
    j = lax.broadcasted_iota(jnp.int32, (count, count), 1)
    normal = normal + jnp.where(i == j, jnp.where(i == DATES - 1, 1.0, damping), 0.0)
    grid[0] = normal[:, :LANES]
    grid[1] = jnp.zeros((count, LANES), jnp.float32)
    grid[1, :, : count - LANES] = normal[:, LANES:]
    lane = lax.broadcasted_iota(jnp.int32, (1, LANES), 1)
    for first in range(0, count, 32):
        rows = min(first + 32 + REACH, count)
        tiles = range(1 if rows <= LANES else 2)
        half = first // LANES

        def sweep(k, carry):
            here = k - half * LANES
            picked = lane == here
            lines = [grid[t, pl.ds(k, 1), :] for t in tiles]
            values = [grid[t, :rows, :] for t in tiles]
            index = jnp.full((rows, LANES), here, jnp.int32)
            column = jnp.take_along_axis(values[half], index, axis=1)
            scale = 1.0 / jnp.take_along_axis(jnp.broadcast_to(lines[half], (8, LANES)), index[:8], axis=1)[:1]
            lines = [line * scale for line in lines]
            lines[half] = jnp.where(picked, -scale, lines[half])
            values[half] = jnp.where(picked, 0.0, values[half])
            for t in tiles:
                grid[t, :rows, :] = values[t] - column * lines[t]
            for t in tiles:
                grid[t, pl.ds(k, 1), :] = lines[t]
            return carry

        lax.fori_loop(first, first + 32, sweep, 0)
    swept = jnp.concatenate([grid[0], grid[1, :, : count - LANES]], axis=1)
    inverse[...] = -jnp.dot(
        swept, counted, precision=lax.Precision.HIGHEST, preferred_element_type=jnp.float32
    )


def network_solve(flip, dates, slots, after=()):
    pairs = dates.shape[1]
    smem = pl.BlockSpec(memory_space=pltpu.SMEM)
    outputs = [
        jax.ShapeDtypeStruct((DATES, pairs), jnp.float32),
        jax.ShapeDtypeStruct((pairs, DATES), jnp.float32),
    ]
    return pl.pallas_call(
        functools.partial(network_kernel, slots=slots),
        grid=(1,),
        in_specs=[smem, whole(dates)] + [pl.BlockSpec(memory_space=pl.ANY)] * len(after),
        out_specs=[whole(x) for x in outputs],
        out_shape=outputs,
        scratch_shapes=[pltpu.VMEM((2, DATES, LANES), jnp.float32)],
        compiler_params=pltpu.CompilerParams(vmem_limit_bytes=VMEM_BYTES),
        cost_estimate=lasting(0.02),
        name="network_solve",
    )(flip, dates, *after)


def invert_kernel(group, looked, inverse, design, *refs):
    *residuals, history, flat, held = refs[-GROUPS - 3 :]
    slots = residuals[0].shape[0]
    count = GROUPS * slots
    rows = looked.reshape(count * 8, LANES)
    for j in range(8):
        flat[:, j * LANES : (j + 1) * LANES] = rows[pl.ds(j, count, stride=8), :]
    phase = flat[...]

    def product(a, b):
        return jnp.dot(a, b, precision=lax.Precision.HIGHEST, preferred_element_type=jnp.float32)

    solved = product(inverse[...], phase)
    blocks = history.shape[0]
    history[:, :32] = jnp.transpose(solved[:LANES]).reshape(blocks, 32, LANES)
    last = DATES - LANES
    tail = jnp.concatenate([solved[LANES:], jnp.zeros((LANES - last, 8 * LANES), jnp.float32)])
    tail = jnp.transpose(tail).reshape(blocks, 4, 8, LANES)
    packed = tail[:, 0]
    for b in range(1, 4):
        packed = packed + pltpu.roll(tail[:, b], b * last, 2)
    history[:, 32:] = packed
    signs = design[...].astype(jnp.bfloat16)
    rest, left = phase, solved
    for _ in range(3):
        part = left.astype(jnp.bfloat16)
        left = left - part.astype(jnp.float32)
        rest = rest - jnp.dot(signs, part, preferred_element_type=jnp.float32)
    lines = held.reshape(count * 8, LANES)
    for j in range(8):
        lines[pl.ds(j, count, stride=8), :] = rest[:, j * LANES : (j + 1) * LANES]
    for d, residual in enumerate(residuals):
        residual[...] = held[pl.ds(jnp.bitwise_xor(group[0], d) * slots, slots)]


def invert(group, looked, inverse, design, after):
    slots = looked.shape[1]
    part = jax.ShapeDtypeStruct((slots, 8, LANES), jnp.float32)
    outputs = [part] * GROUPS + [jax.ShapeDtypeStruct((8 * LANES // 32, 40, LANES), jnp.float32)]
    return pl.pallas_call(
        invert_kernel,
        grid=(1,),
        in_specs=[pl.BlockSpec(memory_space=pltpu.SMEM)]
        + [whole(x) for x in (looked, inverse, design)]
        + [pl.BlockSpec(memory_space=pl.ANY)] * len(after),
        out_specs=[whole(x) for x in outputs],
        out_shape=outputs,
        scratch_shapes=[
            pltpu.VMEM((GROUPS * slots, 8 * LANES), jnp.float32),
            pltpu.VMEM((GROUPS * slots, 8, LANES), jnp.float32),
        ],
        compiler_params=pltpu.CompilerParams(vmem_limit_bytes=VMEM_BYTES),
        cost_estimate=lasting(0.02),
        name="invert",
    )(group, looked, inverse, design, *after)


def unpack_kernel(held, out):
    last = DATES - LANES
    out[:, :, :LANES] = held[:, :32]
    packed = held[:, 32:]
    for b in range(4):
        value = packed if b == 0 else pltpu.roll(packed, LANES - b * last, 2)
        out[:, 8 * b : 8 * (b + 1), LANES:] = value[:, :, : last - 1]


def unpack(held):
    output = jax.ShapeDtypeStruct((held.shape[0], 32, DATES - 1), jnp.float32)
    return pl.pallas_call(
        unpack_kernel,
        grid=(1,),
        in_specs=[whole(held)],
        out_specs=whole(output),
        out_shape=output,
        compiler_params=pltpu.CompilerParams(vmem_limit_bytes=8 * 1024 * 1024),
        cost_estimate=lasting(0.3),
        name="unpack",
    )(held)


def tiles(samples):
    ifgs, az, cols = samples.shape
    split = samples.reshape(ifgs, az, cols // LANES, LANES).transpose(0, 2, 1, 3)
    return split.reshape(ifgs * cols // (LANES * RG_LOOKS), PIECES, LANES)


def local(phase_samples, sample_weights, reference_date, secondary_date, window_rows, window_cols):
    ifgs = phase_samples.shape[0]
    row_count = lax.axis_size("rows")
    odd = lax.rem(lax.axis_index("rows"), 2)
    share = (ifgs + 1) // 2
    rest = ifgs - share
    mates = [(r, r ^ 1) for r in range(row_count)]
    outward = [(r, r + 2 if r % 2 else r - 2) for r in range(row_count)]
    outward = [(s, d) for s, d in outward if 0 <= d < row_count]
    across = [(r, r - 2 if r % 2 else r + 2) for r in range(row_count)]
    across = [(s, d) for s, d in across if 0 <= d < row_count]

    group = lax.axis_index("ifg")
    phase = tiles(phase_samples)
    weight = tiles(sample_weights)
    pool = pooling_matrix()
    flip = (1 - 2 * odd).reshape(1)
    side = odd.reshape(1)
    mine = rest * 32 * odd
    other = rest * 32 * (1 - odd)
    slots = 2 * share
    early = FIRST
    late = share - early

    sent_a, looked = look_sums(
        other.reshape(1), early, early // 2, 0, slots, phase, weight, pool
    )
    mate_a = lax.ppermute(sent_a, "rows", mates)
    sent_b, looked = look_sums(
        (other + early * 32).reshape(1), late, late // 2, early, slots, phase, weight, pool, looked
    )
    mate_b = lax.ppermute(sent_b, "rows", mates)
    own_a, looked = look_sums(
        mine.reshape(1), early, early // 2, share, slots, phase, weight, pool, looked
    )
    far_a = lax.ppermute(own_a, "rows", outward)
    own_b, looked = look_sums(
        (mine + early * 32).reshape(1), late, late // 2, share + early, slots,
        phase, weight, pool, looked, (mate_a,),
    )
    far_b = lax.ppermute(own_b, "rows", outward)
    near_a = lax.ppermute(mate_a, "rows", across)
    moved = lax.all_to_all(looked, "ifg", split_axis=0, concat_axis=0, tiled=True)

    dates = jnp.stack([reference_date, secondary_date]).reshape(2, GROUPS, ifgs)
    dates = jnp.where(
        odd == 0,
        jnp.concatenate([dates[:, :, rest:], dates[:, :, :share]], axis=2),
        jnp.concatenate([dates[:, :, :share], dates[:, :, rest:]], axis=2),
    ).reshape(2, -1)
    offsets = (window_rows, window_cols, flip)
    near_b = lax.ppermute(mate_b, "rows", across)
    own_part_a, mate_part_a = window_coherence(
        offsets, near_a, own_a, mate_a, far_a
    )
    back_a = lax.ppermute(mate_part_a, "rows", mates)
    inverse, design = network_solve(flip, dates, slots, (mate_b, mate_part_a))
    *residual, history = invert(
        group.reshape(1), moved, inverse, design, (back_a,)
    )
    residual = residual[:1] + [
        lax.ppermute(residual[d], "ifg", [(i, i ^ d) for i in range(GROUPS)])
        for d in range(1, GROUPS)
    ]
    own_part_b, mate_part_b = window_coherence(
        offsets, near_b, own_b, mate_b, far_b, after=(residual[1], history)
    )
    back_b = lax.ppermute(mate_part_b, "rows", mates)

    residual = unslot(jnp.stack([odd, group]), ifgs, residual, ())
    by_ifg = (-1, 32, LANES)
    coherence = merge(
        side, ifgs, *[part.reshape(by_ifg) for part in (own_part_a, own_part_b, back_a, back_b)],
        after=(residual,),
    )

    history = lax.all_to_all(history, "rows", split_axis=0, concat_axis=0, tiled=True)
    shape = (ifgs, 1, 32 * LANES)
    return (coherence.reshape(shape), residual.reshape(shape), unpack(history).transpose(2, 0, 1))


def solution(mesh):
    placed = (P("ifg", "rows", None), P("ifg", "rows", None), P(), P(), P(), P())
    return jax.shard_map(
        local,
        mesh=mesh,
        in_specs=placed,
        out_specs=(P("ifg", "rows", None), P("ifg", "rows", None), P(None, None, ("ifg", "rows"))),
        check_vma=False,
    )
```

```python
import functools
import math

import jax
import jax.numpy as jnp
import numpy as np
from jax import lax
from jax.experimental import pallas as pl
from jax.experimental.pallas import tpu as pltpu
from jax.sharding import PartitionSpec as P

DATES = 160
AZ_LOOKS = 2
RG_LOOKS = 8
REACH = 24
OFFSETS = 9
LANES = 128

damping = 0.25

SIN_QUARTER = (
    0.3535533845424652,
    -0.0036828448064625263,
    1.1508434909046628e-05,
    -1.7096880355893518e-08,
    1.4046378643550739e-11,
)
COS_QUARTER = (
    0.9999999403953552,
    -0.031249957159161568,
    0.00016275106463581324,
    -3.383578359716921e-07,
    3.553040917037009e-10,
)
SIN_SCALE = 2.0 * math.sqrt(2.0)

PIECES = 16
PITCH = 17
VMEM_BYTES = 60 * 1024 * 1024
GROUPS = 4
FIRST = 20
GROUP = 16


def pooling_matrix():
    look = np.arange(LANES * RG_LOOKS) // RG_LOOKS
    return jnp.asarray(look[:, None] == np.arange(LANES), jnp.bfloat16)


def lasting(us):
    return pl.CostEstimate(flops=0, bytes_accessed=int(us * 3.6e6), transcendentals=0)


def whole(x):
    zeros = (0,) * len(x.shape)
    return pl.BlockSpec(x.shape, lambda i: zeros)


def horner(coefficients, z):
    total = coefficients[-1] * z + coefficients[-2]
    for c in coefficients[-3::-1]:
        total = total * z + c
    return total


def regroup(ref, held, rows):
    tiles = ref[rows].astype(jnp.float32)
    for m in range(GROUP):
        held[m * PITCH : m * PITCH + PIECES, :] = tiles[m]


def piece(held, q):
    return held[pl.ds(q, GROUP, stride=PITCH), :]


def split_store(high, low, rows, c, value):
    top = value.astype(jnp.bfloat16)
    high[rows, c * LANES : (c + 1) * LANES] = top
    low[rows, c * LANES : (c + 1) * LANES] = (value - top.astype(jnp.float32)).astype(jnp.bfloat16)


def pooled(high, low, pool):
    return jnp.dot(high[...], pool[...], preferred_element_type=jnp.float32) + jnp.dot(
        low[...], pool[...], preferred_element_type=jnp.float32
    )


def look_kernel(start, phase, weight, pool, *refs):
    out, looked, p_held, w_held, wh, wl, ph, plo, sh, sl, qh, ql = refs[-12:]
    block = phase.shape[0]

    def step(g, carry):
        rows = pl.ds(pl.multiple_of(g * GROUP, GROUP), GROUP)
        regroup(phase, p_held, rows)
        regroup(weight, w_held, rows)
        for c in range(RG_LOOKS):
            sums = None
            for a in range(AZ_LOOKS):
                x = piece(p_held, 2 * c + a)
                w = piece(w_held, 2 * c + a)
                z = x * x
                s = x * horner(SIN_QUARTER, z)
                k = horner(COS_QUARTER, z)
                half = s * k
                terms = (w, w * x, w * (half * (1.0 - s * s)), w * (half * half))
                sums = terms if sums is None else [t + u for t, u in zip(sums, terms)]
            for value, high, low in zip(sums, (wh, ph, sh, qh), (wl, plo, sl, ql)):
                split_store(high, low, rows, c, value)
        return carry

    lax.fori_loop(0, block // GROUP, step, 0)
    total = pooled(wh, wl, pool)
    mean = pooled(ph, plo, pool) / total
    looked[...] = jnp.transpose(mean.reshape(block // 32, GROUPS, 8, LANES), (1, 0, 2, 3))
    out[0] = total - 4.0 * pooled(qh, ql, pool)
    out[1] = SIN_SCALE * pooled(sh, sl, pool)
    out[2] = total


def look_sums(start, count, block, slot, slots, phase, weight, pool, looked=None, after=()):
    element = pl.Element
    rows = block * 32
    samples = pl.BlockSpec(
        (element(rows), element(PIECES), element(LANES)),
        lambda i, s: (pl.multiple_of(s[0] + i * rows, 16), 0, 0),
    )
    operands = [phase, weight, pool]
    in_specs = [samples, samples, pl.BlockSpec(pool.shape, lambda i, s: (0, 0))]
    aliases = {}
    if looked is not None:
        operands.append(looked)
        in_specs.append(pl.BlockSpec(memory_space=pl.ANY))
        aliases = {4: 1}
    operands.extend(after)
    in_specs.extend([pl.BlockSpec(memory_space=pl.ANY)] * len(after))
    return pl.pallas_call(
        look_kernel,
        grid_spec=pltpu.PrefetchScalarGridSpec(
            num_scalar_prefetch=1,
            grid=(count // block,),
            in_specs=in_specs,
            out_specs=[
                pl.BlockSpec((3, rows, LANES), lambda i, s: (0, i, 0)),
                pl.BlockSpec(
                    (element(GROUPS), element(block), element(8), element(LANES)),
                    lambda i, s: (0, slot + i * block, 0, 0),
                ),
            ],
            scratch_shapes=[pltpu.VMEM((GROUP * PITCH + 16, LANES), jnp.float32)] * 2
            + [pltpu.VMEM((rows, RG_LOOKS * LANES), jnp.bfloat16)] * 8,
        ),
        out_shape=[
            jax.ShapeDtypeStruct((3, count * 32, LANES), jnp.float32),
            jax.ShapeDtypeStruct((GROUPS, slots, 8, LANES), jnp.float32),
        ],
        input_output_aliases=aliases,
        compiler_params=pltpu.CompilerParams(vmem_limit_bytes=56 * 1024 * 1024),
        cost_estimate=lasting(0.02),
        name="look_sums",
    )(start, *operands)


def window_kernel(row_off, col_off, flip, near, own, mate, far, *refs):
    own_out, mate_out, parts, bands = refs[-4:]
    rows = own.shape[1]

    @pl.when(pl.program_id(0) == 0)
    def _():
        window_bands(row_off, col_off, flip, bands)

    def divide(g, carry):
        r = pl.ds(pl.multiple_of(g * 32, 32), 32)
        for source, ref in enumerate((near, own, mate, far)):
            for quantity in range(3):
                value = ref[quantity, r, :]
                high = value.astype(jnp.bfloat16)
                low = (value - high.astype(jnp.float32)).astype(jnp.bfloat16)
                at = source * 2 * LANES
                parts[quantity, r, at : at + LANES] = high
                parts[quantity, r, at + LANES : at + 2 * LANES] = low
        return carry

    lax.fori_loop(0, rows // 32, divide, 0)
    lane = lax.broadcasted_iota(jnp.int32, (rows, LANES), 1)
    row = lax.rem(lax.broadcasted_iota(jnp.int32, (rows, LANES), 0), 32)
    upper = lane >= LANES // 2
    valid = (upper & (row < 31)) | (jnp.logical_not(upper) & (row > 0))
    for side, out in enumerate((own_out, mate_out)):
        sums = []
        for quantity in range(3):
            left = parts[quantity, :, side * 2 * LANES : (side + 3) * 2 * LANES]
            both = jnp.dot(left, bands[...], preferred_element_type=jnp.float32)
            edge = both[:, LANES:]
            edge = jnp.where(upper, pltpu.roll(edge, rows - 1, 0), pltpu.roll(edge, 1, 0))
            sums.append(both[:, :LANES] + jnp.where(valid, edge, 0.0))
        re, im, w = sums
        out[...] = jnp.sqrt(re * re + im * im) / w


def window_coherence(offsets, near, own, mate, far, after=()):
    count = mate.shape[1]
    rows = count // 2
    part = pl.BlockSpec((3, rows, LANES), lambda i: (0, i, 0))
    out = pl.BlockSpec((rows, LANES), lambda i: (i, 0))
    return pl.pallas_call(
        window_kernel,
        grid=(2,),
        in_specs=[pl.BlockSpec(memory_space=pltpu.SMEM)] * 3
        + [part] * 4
        + [pl.BlockSpec(memory_space=pl.ANY)] * len(after),
        out_specs=[out, out],
        out_shape=[jax.ShapeDtypeStruct((count, LANES), jnp.float32)] * 2,
        scratch_shapes=[
            pltpu.VMEM((3, rows, 8 * LANES), jnp.bfloat16),
            pltpu.VMEM((6 * LANES, 2 * LANES), jnp.bfloat16),
        ],
        compiler_params=pltpu.CompilerParams(vmem_limit_bytes=24 * 1024 * 1024),
        cost_estimate=lasting(0.02),
        name="window_coherence",
    )(*offsets, near, own, mate, far, *after)


def merge_kernel(odd, own_a, own_b, other_a, other_b, *refs):
    out = refs[-1]
    first, share = own_a.shape[0], own_a.shape[0] + own_b.shape[0]

    @pl.when(odd[0] == 0)
    def _():
        out[:first] = own_a[...]
        out[first:share] = own_b[...]
        out[share : share + first - 1] = other_a[1:]
        out[share + first - 1 :] = other_b[...]

    @pl.when(odd[0] != 0)
    def _():
        out[:first] = other_a[...]
        out[first:share] = other_b[...]
        out[share : share + first - 1] = own_a[1:]
        out[share + first - 1 :] = own_b[...]


def merge(odd, ifgs, *parts, after):
    output = jax.ShapeDtypeStruct((ifgs, *parts[0].shape[1:]), jnp.float32)
    return pl.pallas_call(
        merge_kernel,
        grid=(1,),
        in_specs=[pl.BlockSpec(memory_space=pltpu.SMEM)]
        + [whole(x) for x in parts]
        + [pl.BlockSpec(memory_space=pl.ANY)] * len(after),
        out_specs=whole(output),
        out_shape=output,
        compiler_params=pltpu.CompilerParams(vmem_limit_bytes=24 * 1024 * 1024),
        cost_estimate=lasting(0.3),
        name="merge",
    )(odd, *parts, *after)


def unslot_kernel(where, *refs):
    parts, out = refs[:GROUPS], refs[-1]
    share = parts[0].shape[0] // 2
    rest = out.shape[0] - share
    odd = where[0]
    for d, part in enumerate(parts):
        chunk = pl.ds(jnp.bitwise_xor(where[1], d), 1)
        out[:share, chunk] = part[pl.ds(share * (1 - odd), share)][:, None]
        out[share:, chunk] = part[pl.ds(1 + share * odd, rest)][:, None]


def unslot(where, ifgs, parts, after):
    output = jax.ShapeDtypeStruct((ifgs, GROUPS, *parts[0].shape[1:]), jnp.float32)
    return pl.pallas_call(
        unslot_kernel,
        grid=(1,),
        in_specs=[pl.BlockSpec(memory_space=pltpu.SMEM)]
        + [whole(x) for x in parts]
        + [pl.BlockSpec(memory_space=pl.ANY)] * len(after),
        out_specs=whole(output),
        out_shape=output,
        compiler_params=pltpu.CompilerParams(vmem_limit_bytes=24 * 1024 * 1024),
        cost_estimate=lasting(50),
        name="unslot",
    )(where, *parts, *after)


def window_bands(row_off, col_off, flip, bands):
    gap = lax.broadcasted_iota(jnp.int32, (LANES, LANES), 1) - lax.broadcasted_iota(
        jnp.int32, (LANES, LANES), 0
    )
    for e in range(3):
        same = jnp.zeros((LANES, LANES), jnp.float32)
        next_to = jnp.zeros((LANES, LANES), jnp.float32)
        for k in range(OFFSETS):
            amount = jnp.where(row_off[k] * flip[0] == e - 1, 1.0, 0.0)
            moved = gap + col_off[k]
            same = same + jnp.where(moved == 0, amount, 0.0)
            next_to = next_to + jnp.where(jnp.abs(moved) == LANES, amount, 0.0)
        for half in range(2):
            rows = slice((2 * e + half) * LANES, (2 * e + half + 1) * LANES)
            bands[rows, :LANES] = same.astype(jnp.bfloat16)
            bands[rows, LANES:] = next_to.astype(jnp.bfloat16)


def network_kernel(
    flip, dates, *refs, slots
):
    inverse, design, grid = refs[-3:]
    count = inverse.shape[0]
    date = lax.broadcasted_iota(jnp.int32, inverse.shape, 0) + 1
    signed = (dates[1:2] == date).astype(jnp.float32) - (dates[0:1] == date).astype(jnp.float32)
    design[...] = jnp.transpose(signed)
    slot = lax.rem(lax.broadcasted_iota(jnp.int32, inverse.shape, 1), slots)
    again = jnp.where(flip[0] > 0, 0, slots // 2 - 1)
    counted = jnp.where(slot == again, 0.0, signed)
    normal = lax.dot_general(
        counted.astype(jnp.bfloat16), signed.astype(jnp.bfloat16), (((1,), (1,)), ((), ())), preferred_element_type=jnp.float32
    )
    i = lax.broadcasted_iota(jnp.int32, (count, count), 0)
    j = lax.broadcasted_iota(jnp.int32, (count, count), 1)
    normal = normal + jnp.where(i == j, jnp.where(i == DATES - 1, 1.0, damping), 0.0)
    grid[0] = normal[:, :LANES]
    grid[1] = jnp.zeros((count, LANES), jnp.float32)
    grid[1, :, : count - LANES] = normal[:, LANES:]
    lane = lax.broadcasted_iota(jnp.int32, (1, LANES), 1)
    for first in range(0, count, 32):
        rows = min(first + 32 + REACH, count)
        tiles = range(1 if rows <= LANES else 2)
        half = first // LANES

        def sweep(k, carry):
            here = k - half * LANES
            picked = lane == here
            lines = [grid[t, pl.ds(k, 1), :] for t in tiles]
            values = [grid[t, :rows, :] for t in tiles]
            index = jnp.full((rows, LANES), here, jnp.int32)
            column = jnp.take_along_axis(values[half], index, axis=1)
            scale = 1.0 / jnp.take_along_axis(jnp.broadcast_to(lines[half], (8, LANES)), index[:8], axis=1)[:1]
            lines = [line * scale for line in lines]
            lines[half] = jnp.where(picked, -scale, lines[half])
            values[half] = jnp.where(picked, 0.0, values[half])
            for t in tiles:
                grid[t, :rows, :] = values[t] - column * lines[t]
            for t in tiles:
                grid[t, pl.ds(k, 1), :] = lines[t]
            return carry

        lax.fori_loop(first, first + 32, sweep, 0)
    swept = jnp.concatenate([grid[0], grid[1, :, : count - LANES]], axis=1)
    inverse[...] = -jnp.dot(
        swept, counted, precision=lax.Precision.HIGHEST, preferred_element_type=jnp.float32
    )


def network_solve(flip, dates, slots, after=()):
    pairs = dates.shape[1]
    smem = pl.BlockSpec(memory_space=pltpu.SMEM)
    outputs = [
        jax.ShapeDtypeStruct((DATES, pairs), jnp.float32),
        jax.ShapeDtypeStruct((pairs, DATES), jnp.float32),
    ]
    return pl.pallas_call(
        functools.partial(network_kernel, slots=slots),
        grid=(1,),
        in_specs=[smem, whole(dates)] + [pl.BlockSpec(memory_space=pl.ANY)] * len(after),
        out_specs=[whole(x) for x in outputs],
        out_shape=outputs,
        scratch_shapes=[pltpu.VMEM((2, DATES, LANES), jnp.float32)],
        compiler_params=pltpu.CompilerParams(vmem_limit_bytes=VMEM_BYTES),
        cost_estimate=lasting(0.02),
        name="network_solve",
    )(flip, dates, *after)


def invert_kernel(group, looked, inverse, design, *refs):
    *residuals, history, flat, held = refs[-GROUPS - 3 :]
    slots = residuals[0].shape[0]
    count = GROUPS * slots
    rows = looked.reshape(count * 8, LANES)
    for j in range(8):
        flat[:, j * LANES : (j + 1) * LANES] = rows[pl.ds(j, count, stride=8), :]
    phase = flat[...]

    def product(a, b):
        return jnp.dot(a, b, precision=lax.Precision.HIGHEST, preferred_element_type=jnp.float32)

    solved = product(inverse[...], phase)
    blocks = history.shape[0]
    history[:, :32] = jnp.transpose(solved[:LANES]).reshape(blocks, 32, LANES)
    last = DATES - LANES
    tail = jnp.concatenate([solved[LANES:], jnp.zeros((LANES - last, 8 * LANES), jnp.float32)])
    tail = jnp.transpose(tail).reshape(blocks, 4, 8, LANES)
    packed = tail[:, 0]
    for b in range(1, 4):
        packed = packed + pltpu.roll(tail[:, b], b * last, 2)
    history[:, 32:] = packed
    signs = design[...].astype(jnp.bfloat16)
    rest, left = phase, solved
    for _ in range(3):
        part = left.astype(jnp.bfloat16)
        left = left - part.astype(jnp.float32)
        rest = rest - jnp.dot(signs, part, preferred_element_type=jnp.float32)
    lines = held.reshape(count * 8, LANES)
    for j in range(8):
        lines[pl.ds(j, count, stride=8), :] = rest[:, j * LANES : (j + 1) * LANES]
    for d, residual in enumerate(residuals):
        residual[...] = held[pl.ds(jnp.bitwise_xor(group[0], d) * slots, slots)]


def invert(group, looked, inverse, design, after):
    slots = looked.shape[1]
    part = jax.ShapeDtypeStruct((slots, 8, LANES), jnp.float32)
    outputs = [part] * GROUPS + [jax.ShapeDtypeStruct((8 * LANES // 32, 40, LANES), jnp.float32)]
    return pl.pallas_call(
        invert_kernel,
        grid=(1,),
        in_specs=[pl.BlockSpec(memory_space=pltpu.SMEM)]
        + [whole(x) for x in (looked, inverse, design)]
        + [pl.BlockSpec(memory_space=pl.ANY)] * len(after),
        out_specs=[whole(x) for x in outputs],
        out_shape=outputs,
        scratch_shapes=[
            pltpu.VMEM((GROUPS * slots, 8 * LANES), jnp.float32),
            pltpu.VMEM((GROUPS * slots, 8, LANES), jnp.float32),
        ],
        compiler_params=pltpu.CompilerParams(vmem_limit_bytes=VMEM_BYTES),
        cost_estimate=lasting(0.02),
        name="invert",
    )(group, looked, inverse, design, *after)


def unpack_kernel(held, out):
    last = DATES - LANES
    out[:, :, :LANES] = held[:, :32]
    packed = held[:, 32:]
    for b in range(4):
        value = packed if b == 0 else pltpu.roll(packed, LANES - b * last, 2)
        out[:, 8 * b : 8 * (b + 1), LANES:] = value[:, :, : last - 1]


def unpack(held):
    output = jax.ShapeDtypeStruct((held.shape[0], 32, DATES - 1), jnp.float32)
    return pl.pallas_call(
        unpack_kernel,
        grid=(1,),
        in_specs=[whole(held)],
        out_specs=whole(output),
        out_shape=output,
        compiler_params=pltpu.CompilerParams(vmem_limit_bytes=8 * 1024 * 1024),
        cost_estimate=lasting(0.3),
        name="unpack",
    )(held)


def tiles(samples):
    ifgs, az, cols = samples.shape
    split = samples.reshape(ifgs, az, cols // LANES, LANES).transpose(0, 2, 1, 3)
    return split.reshape(ifgs * cols // (LANES * RG_LOOKS), PIECES, LANES)


def local(phase_samples, sample_weights, reference_date, secondary_date, window_rows, window_cols):
    ifgs = phase_samples.shape[0]
    row_count = lax.axis_size("rows")
    odd = lax.rem(lax.axis_index("rows"), 2)
    share = (ifgs + 1) // 2
    rest = ifgs - share
    mates = [(r, r ^ 1) for r in range(row_count)]
    outward = [(r, r + 2 if r % 2 else r - 2) for r in range(row_count)]
    outward = [(s, d) for s, d in outward if 0 <= d < row_count]
    across = [(r, r - 2 if r % 2 else r + 2) for r in range(row_count)]
    across = [(s, d) for s, d in across if 0 <= d < row_count]

    group = lax.axis_index("ifg")
    phase = tiles(phase_samples)
    weight = tiles(sample_weights)
    pool = pooling_matrix()
    flip = (1 - 2 * odd).reshape(1)
    side = odd.reshape(1)
    mine = rest * 32 * odd
    other = rest * 32 * (1 - odd)
    slots = 2 * share
    early = FIRST
    late = share - early

    sent_a, looked = look_sums(
        other.reshape(1), early, early // 2, 0, slots, phase, weight, pool
    )
    mate_a = lax.ppermute(sent_a, "rows", mates)
    sent_b, looked = look_sums(
        (other + early * 32).reshape(1), late, late // 2, early, slots, phase, weight, pool, looked
    )
    mate_b = lax.ppermute(sent_b, "rows", mates)
    own_a, looked = look_sums(
        mine.reshape(1), early, early // 2, share, slots, phase, weight, pool, looked
    )
    far_a = lax.ppermute(own_a, "rows", outward)
    own_b, looked = look_sums(
        (mine + early * 32).reshape(1), late, late // 2, share + early, slots,
        phase, weight, pool, looked, (mate_a,),
    )
    far_b = lax.ppermute(own_b, "rows", outward)
    near_a = lax.ppermute(mate_a, "rows", across)
    moved = lax.all_to_all(looked, "ifg", split_axis=0, concat_axis=0, tiled=True)

    dates = jnp.stack([reference_date, secondary_date]).reshape(2, GROUPS, ifgs)
    dates = jnp.where(
        odd == 0,
        jnp.concatenate([dates[:, :, rest:], dates[:, :, :share]], axis=2),
        jnp.concatenate([dates[:, :, :share], dates[:, :, rest:]], axis=2),
    ).reshape(2, -1)
    offsets = (window_rows, window_cols, flip)
    near_b = lax.ppermute(mate_b, "rows", across)
    own_part_a, mate_part_a = window_coherence(
        offsets, near_a, own_a, mate_a, far_a
    )
    back_a = lax.ppermute(mate_part_a, "rows", mates)
    inverse, design = network_solve(flip, dates, slots, (mate_b, mate_part_a))
    *residual, history = invert(
        group.reshape(1), moved, inverse, design, (back_a,)
    )
    residual = residual[:1] + [
        lax.ppermute(residual[d], "ifg", [(i, i ^ d) for i in range(GROUPS)])
        for d in range(1, GROUPS)
    ]
    own_part_b, mate_part_b = window_coherence(
        offsets, near_b, own_b, mate_b, far_b, after=(residual[1], history)
    )
    back_b = lax.ppermute(mate_part_b, "rows", mates)

    residual = unslot(jnp.stack([odd, group]), ifgs, residual, ())
    by_ifg = (-1, 32, LANES)
    coherence = merge(
        side, ifgs, *[part.reshape(by_ifg) for part in (own_part_a, own_part_b, back_a, back_b)],
        after=(residual,),
    )

    history = lax.all_to_all(history, "rows", split_axis=0, concat_axis=0, tiled=True)
    shape = (ifgs, 1, 32 * LANES)
    return (coherence.reshape(shape), residual.reshape(shape), unpack(history).transpose(2, 0, 1))


def solution(mesh):
    placed = (P("ifg", "rows", None), P("ifg", "rows", None), P(), P(), P(), P())
    return jax.shard_map(
        local,
        mesh=mesh,
        in_specs=placed,
        out_specs=(P("ifg", "rows", None), P("ifg", "rows", None), P(None, None, ("ifg", "rows"))),
        check_vma=False,
    )
```

```python
import functools
import math

import jax
import jax.numpy as jnp
import numpy as np
from jax import lax
from jax.experimental import pallas as pl
from jax.experimental.pallas import tpu as pltpu
from jax.sharding import PartitionSpec as P

DATES = 160
AZ_LOOKS = 2
RG_LOOKS = 8
REACH = 24
OFFSETS = 9
LANES = 128

damping = 0.25

SIN_QUARTER = (
    0.3535533845424652,
    -0.0036828448064625263,
    1.1508434909046628e-05,
    -1.7096880355893518e-08,
    1.4046378643550739e-11,
)
COS_QUARTER = (
    0.9999999403953552,
    -0.031249957159161568,
    0.00016275106463581324,
    -3.383578359716921e-07,
    3.553040917037009e-10,
)
SIN_SCALE = 2.0 * math.sqrt(2.0)

PIECES = 16
PITCH = 17
VMEM_BYTES = 60 * 1024 * 1024
GROUPS = 4
FIRST = 20
GROUP = 16


def pooling_matrix():
    look = np.arange(LANES * RG_LOOKS) // RG_LOOKS
    return jnp.asarray(look[:, None] == np.arange(LANES), jnp.bfloat16)


def lasting(us):
    return pl.CostEstimate(flops=0, bytes_accessed=int(us * 3.6e6), transcendentals=0)


def whole(x):
    zeros = (0,) * len(x.shape)
    return pl.BlockSpec(x.shape, lambda i: zeros)


def horner(coefficients, z):
    total = coefficients[-1] * z + coefficients[-2]
    for c in coefficients[-3::-1]:
        total = total * z + c
    return total


def regroup(ref, held, rows):
    tiles = ref[rows].astype(jnp.float32)
    for m in range(GROUP):
        held[m * PITCH : m * PITCH + PIECES, :] = tiles[m]


def piece(held, q):
    return held[pl.ds(q, GROUP, stride=PITCH), :]


def split_store(high, low, rows, c, value):
    top = value.astype(jnp.bfloat16)
    high[rows, c * LANES : (c + 1) * LANES] = top
    low[rows, c * LANES : (c + 1) * LANES] = (value - top.astype(jnp.float32)).astype(jnp.bfloat16)


def pooled(high, low, pool):
    return jnp.dot(high[...], pool[...], preferred_element_type=jnp.float32) + jnp.dot(
        low[...], pool[...], preferred_element_type=jnp.float32
    )


def look_kernel(start, phase, weight, pool, *refs):
    out, looked, p_held, w_held, wh, wl, ph, plo, sh, sl, qh, ql = refs[-12:]
    block = phase.shape[0]

    def step(g, carry):
        rows = pl.ds(pl.multiple_of(g * GROUP, GROUP), GROUP)
        regroup(phase, p_held, rows)
        regroup(weight, w_held, rows)
        for c in range(RG_LOOKS):
            sums = None
            for a in range(AZ_LOOKS):
                x = piece(p_held, 2 * c + a)
                w = piece(w_held, 2 * c + a)
                z = x * x
                s = x * horner(SIN_QUARTER, z)
                k = horner(COS_QUARTER, z)
                half = s * k
                terms = (w, w * x, w * (half * (1.0 - s * s)), w * (half * half))
                sums = terms if sums is None else [t + u for t, u in zip(sums, terms)]
            for value, high, low in zip(sums, (wh, ph, sh, qh), (wl, plo, sl, ql)):
                split_store(high, low, rows, c, value)
        return carry

    lax.fori_loop(0, block // GROUP, step, 0)
    total = pooled(wh, wl, pool)
    mean = pooled(ph, plo, pool) / total
    looked[...] = jnp.transpose(mean.reshape(block // 32, GROUPS, 8, LANES), (1, 0, 2, 3))
    out[0] = total - 4.0 * pooled(qh, ql, pool)
    out[1] = SIN_SCALE * pooled(sh, sl, pool)
    out[2] = total


def look_sums(start, count, block, slot, slots, phase, weight, pool, looked=None, after=()):
    element = pl.Element
    rows = block * 32
    samples = pl.BlockSpec(
        (element(rows), element(PIECES), element(LANES)),
        lambda i, s: (pl.multiple_of(s[0] + i * rows, 16), 0, 0),
    )
    operands = [phase, weight, pool]
    in_specs = [samples, samples, pl.BlockSpec(pool.shape, lambda i, s: (0, 0))]
    aliases = {}
    if looked is not None:
        operands.append(looked)
        in_specs.append(pl.BlockSpec(memory_space=pl.ANY))
        aliases = {4: 1}
    operands.extend(after)
    in_specs.extend([pl.BlockSpec(memory_space=pl.ANY)] * len(after))
    return pl.pallas_call(
        look_kernel,
        grid_spec=pltpu.PrefetchScalarGridSpec(
            num_scalar_prefetch=1,
            grid=(count // block,),
            in_specs=in_specs,
            out_specs=[
                pl.BlockSpec((3, rows, LANES), lambda i, s: (0, i, 0)),
                pl.BlockSpec(
                    (element(GROUPS), element(block), element(8), element(LANES)),
                    lambda i, s: (0, slot + i * block, 0, 0),
                ),
            ],
            scratch_shapes=[pltpu.VMEM((GROUP * PITCH + 16, LANES), jnp.float32)] * 2
            + [pltpu.VMEM((rows, RG_LOOKS * LANES), jnp.bfloat16)] * 8,
        ),
        out_shape=[
            jax.ShapeDtypeStruct((3, count * 32, LANES), jnp.float32),
            jax.ShapeDtypeStruct((GROUPS, slots, 8, LANES), jnp.float32),
        ],
        input_output_aliases=aliases,
        compiler_params=pltpu.CompilerParams(vmem_limit_bytes=56 * 1024 * 1024),
        cost_estimate=lasting(0.02),
        name="look_sums",
    )(start, *operands)


def window_kernel(row_off, col_off, flip, near, own, mate, far, *refs):
    own_out, mate_out, parts, bands = refs[-4:]
    rows = own.shape[1]

    @pl.when(pl.program_id(0) == 0)
    def _():
        window_bands(row_off, col_off, flip, bands)

    def divide(g, carry):
        r = pl.ds(pl.multiple_of(g * 32, 32), 32)
        for source, ref in enumerate((near, own, mate, far)):
            for quantity in range(3):
                value = ref[quantity, r, :]
                high = value.astype(jnp.bfloat16)
                low = (value - high.astype(jnp.float32)).astype(jnp.bfloat16)
                at = source * 2 * LANES
                parts[quantity, r, at : at + LANES] = high
                parts[quantity, r, at + LANES : at + 2 * LANES] = low
        return carry

    lax.fori_loop(0, rows // 32, divide, 0)
    lane = lax.broadcasted_iota(jnp.int32, (rows, LANES), 1)
    row = lax.rem(lax.broadcasted_iota(jnp.int32, (rows, LANES), 0), 32)
    upper = lane >= LANES // 2
    valid = (upper & (row < 31)) | (jnp.logical_not(upper) & (row > 0))
    for side, out in enumerate((own_out, mate_out)):
        sums = []
        for quantity in range(3):
            left = parts[quantity, :, side * 2 * LANES : (side + 3) * 2 * LANES]
            both = jnp.dot(left, bands[...], preferred_element_type=jnp.float32)
            edge = both[:, LANES:]
            edge = jnp.where(upper, pltpu.roll(edge, rows - 1, 0), pltpu.roll(edge, 1, 0))
            sums.append(both[:, :LANES] + jnp.where(valid, edge, 0.0))
        re, im, w = sums
        out[...] = jnp.sqrt(re * re + im * im) / w


def window_coherence(offsets, near, own, mate, far, after=()):
    count = mate.shape[1]
    rows = count // 2
    part = pl.BlockSpec((3, rows, LANES), lambda i: (0, i, 0))
    out = pl.BlockSpec((rows, LANES), lambda i: (i, 0))
    return pl.pallas_call(
        window_kernel,
        grid=(2,),
        in_specs=[pl.BlockSpec(memory_space=pltpu.SMEM)] * 3
        + [part] * 4
        + [pl.BlockSpec(memory_space=pl.ANY)] * len(after),
        out_specs=[out, out],
        out_shape=[jax.ShapeDtypeStruct((count, LANES), jnp.float32)] * 2,
        scratch_shapes=[
            pltpu.VMEM((3, rows, 8 * LANES), jnp.bfloat16),
            pltpu.VMEM((6 * LANES, 2 * LANES), jnp.bfloat16),
        ],
        compiler_params=pltpu.CompilerParams(vmem_limit_bytes=24 * 1024 * 1024),
        cost_estimate=lasting(0.02),
        name="window_coherence",
    )(*offsets, near, own, mate, far, *after)


def merge_kernel(odd, own_a, own_b, other_a, other_b, *refs):
    out = refs[-1]
    first, share = own_a.shape[0], own_a.shape[0] + own_b.shape[0]

    @pl.when(odd[0] == 0)
    def _():
        out[:first] = own_a[...]
        out[first:share] = own_b[...]
        out[share : share + first - 1] = other_a[1:]
        out[share + first - 1 :] = other_b[...]

    @pl.when(odd[0] != 0)
    def _():
        out[:first] = other_a[...]
        out[first:share] = other_b[...]
        out[share : share + first - 1] = own_a[1:]
        out[share + first - 1 :] = own_b[...]


def merge(odd, ifgs, *parts, after):
    output = jax.ShapeDtypeStruct((ifgs, *parts[0].shape[1:]), jnp.float32)
    return pl.pallas_call(
        merge_kernel,
        grid=(1,),
        in_specs=[pl.BlockSpec(memory_space=pltpu.SMEM)]
        + [whole(x) for x in parts]
        + [pl.BlockSpec(memory_space=pl.ANY)] * len(after),
        out_specs=whole(output),
        out_shape=output,
        compiler_params=pltpu.CompilerParams(vmem_limit_bytes=24 * 1024 * 1024),
        cost_estimate=lasting(0.3),
        name="merge",
    )(odd, *parts, *after)


def unslot_kernel(where, *refs):
    parts, out = refs[:GROUPS], refs[-1]
    share = parts[0].shape[0] // 2
    rest = out.shape[0] - share
    odd = where[0]
    for d, part in enumerate(parts):
        chunk = pl.ds(jnp.bitwise_xor(where[1], d), 1)
        out[:share, chunk] = part[pl.ds(share * (1 - odd), share)][:, None]
        out[share:, chunk] = part[pl.ds(1 + share * odd, rest)][:, None]


def unslot(where, ifgs, parts, after):
    output = jax.ShapeDtypeStruct((ifgs, GROUPS, *parts[0].shape[1:]), jnp.float32)
    return pl.pallas_call(
        unslot_kernel,
        grid=(1,),
        in_specs=[pl.BlockSpec(memory_space=pltpu.SMEM)]
        + [whole(x) for x in parts]
        + [pl.BlockSpec(memory_space=pl.ANY)] * len(after),
        out_specs=whole(output),
        out_shape=output,
        compiler_params=pltpu.CompilerParams(vmem_limit_bytes=24 * 1024 * 1024),
        cost_estimate=lasting(50),
        name="unslot",
    )(where, *parts, *after)


def window_bands(row_off, col_off, flip, bands):
    gap = lax.broadcasted_iota(jnp.int32, (LANES, LANES), 1) - lax.broadcasted_iota(
        jnp.int32, (LANES, LANES), 0
    )
    for e in range(3):
        same = jnp.zeros((LANES, LANES), jnp.float32)
        next_to = jnp.zeros((LANES, LANES), jnp.float32)
        for k in range(OFFSETS):
            amount = jnp.where(row_off[k] * flip[0] == e - 1, 1.0, 0.0)
            moved = gap + col_off[k]
            same = same + jnp.where(moved == 0, amount, 0.0)
            next_to = next_to + jnp.where(jnp.abs(moved) == LANES, amount, 0.0)
        for half in range(2):
            rows = slice((2 * e + half) * LANES, (2 * e + half + 1) * LANES)
            bands[rows, :LANES] = same.astype(jnp.bfloat16)
            bands[rows, LANES:] = next_to.astype(jnp.bfloat16)


def network_kernel(
    flip, dates, *refs, slots
):
    inverse, design, grid = refs[-3:]
    count = inverse.shape[0]
    date = lax.broadcasted_iota(jnp.int32, inverse.shape, 0) + 1
    signed = (dates[1:2] == date).astype(jnp.float32) - (dates[0:1] == date).astype(jnp.float32)
    design[...] = jnp.transpose(signed)
    slot = lax.rem(lax.broadcasted_iota(jnp.int32, inverse.shape, 1), slots)
    again = jnp.where(flip[0] > 0, 0, slots // 2 - 1)
    counted = jnp.where(slot == again, 0.0, signed)
    normal = lax.dot_general(
        counted.astype(jnp.bfloat16), signed.astype(jnp.bfloat16), (((1,), (1,)), ((), ())), preferred_element_type=jnp.float32
    )
    i = lax.broadcasted_iota(jnp.int32, (count, count), 0)
    j = lax.broadcasted_iota(jnp.int32, (count, count), 1)
    normal = normal + jnp.where(i == j, jnp.where(i == DATES - 1, 1.0, damping), 0.0)
    grid[0] = normal[:, :LANES]
    grid[1] = jnp.zeros((count, LANES), jnp.float32)
    grid[1, :, : count - LANES] = normal[:, LANES:]
    lane = lax.broadcasted_iota(jnp.int32, (1, LANES), 1)
    for first in range(0, count, 32):
        rows = min(first + 32 + REACH, count)
        tiles = range(1 if rows <= LANES else 2)
        half = first // LANES

        def sweep(k, carry):
            here = k - half * LANES
            picked = lane == here
            lines = [grid[t, pl.ds(k, 1), :] for t in tiles]
            values = [grid[t, :rows, :] for t in tiles]
            index = jnp.full((rows, LANES), here, jnp.int32)
            column = jnp.take_along_axis(values[half], index, axis=1)
            scale = 1.0 / jnp.take_along_axis(jnp.broadcast_to(lines[half], (8, LANES)), index[:8], axis=1)[:1]
            lines = [line * scale for line in lines]
            lines[half] = jnp.where(picked, -scale, lines[half])
            values[half] = jnp.where(picked, 0.0, values[half])
            for t in tiles:
                grid[t, :rows, :] = values[t] - column * lines[t]
            for t in tiles:
                grid[t, pl.ds(k, 1), :] = lines[t]
            return carry

        lax.fori_loop(first, first + 32, sweep, 0)
    swept = jnp.concatenate([grid[0], grid[1, :, : count - LANES]], axis=1)
    inverse[...] = -jnp.dot(
        swept, counted, precision=lax.Precision.HIGHEST, preferred_element_type=jnp.float32
    )


def network_solve(flip, dates, slots, after=()):
    pairs = dates.shape[1]
    smem = pl.BlockSpec(memory_space=pltpu.SMEM)
    outputs = [
        jax.ShapeDtypeStruct((DATES, pairs), jnp.float32),
        jax.ShapeDtypeStruct((pairs, DATES), jnp.float32),
    ]
    return pl.pallas_call(
        functools.partial(network_kernel, slots=slots),
        grid=(1,),
        in_specs=[smem, whole(dates)] + [pl.BlockSpec(memory_space=pl.ANY)] * len(after),
        out_specs=[whole(x) for x in outputs],
        out_shape=outputs,
        scratch_shapes=[pltpu.VMEM((2, DATES, LANES), jnp.float32)],
        compiler_params=pltpu.CompilerParams(vmem_limit_bytes=VMEM_BYTES),
        cost_estimate=lasting(0.02),
        name="network_solve",
    )(flip, dates, *after)


def invert_kernel(group, looked, inverse, design, *refs):
    *residuals, history, flat, held = refs[-GROUPS - 3 :]
    slots = residuals[0].shape[0]
    count = GROUPS * slots
    rows = looked.reshape(count * 8, LANES)
    for j in range(8):
        flat[:, j * LANES : (j + 1) * LANES] = rows[pl.ds(j, count, stride=8), :]
    phase = flat[...]

    def product(a, b):
        return jnp.dot(a, b, precision=lax.Precision.HIGHEST, preferred_element_type=jnp.float32)

    solved = product(inverse[...], phase)
    blocks = history.shape[0]
    history[:, :32] = jnp.transpose(solved[:LANES]).reshape(blocks, 32, LANES)
    last = DATES - LANES
    tail = jnp.concatenate([solved[LANES:], jnp.zeros((LANES - last, 8 * LANES), jnp.float32)])
    tail = jnp.transpose(tail).reshape(blocks, 4, 8, LANES)
    packed = tail[:, 0]
    for b in range(1, 4):
        packed = packed + pltpu.roll(tail[:, b], b * last, 2)
    history[:, 32:] = packed
    signs = design[...].astype(jnp.bfloat16)
    rest, left = phase, solved
    for _ in range(3):
        part = left.astype(jnp.bfloat16)
        left = left - part.astype(jnp.float32)
        rest = rest - jnp.dot(signs, part, preferred_element_type=jnp.float32)
    lines = held.reshape(count * 8, LANES)
    for j in range(8):
        lines[pl.ds(j, count, stride=8), :] = rest[:, j * LANES : (j + 1) * LANES]
    for d, residual in enumerate(residuals):
        residual[...] = held[pl.ds(jnp.bitwise_xor(group[0], d) * slots, slots)]


def invert(group, looked, inverse, design, after):
    slots = looked.shape[1]
    part = jax.ShapeDtypeStruct((slots, 8, LANES), jnp.float32)
    outputs = [part] * GROUPS + [jax.ShapeDtypeStruct((8 * LANES // 32, 40, LANES), jnp.float32)]
    return pl.pallas_call(
        invert_kernel,
        grid=(1,),
        in_specs=[pl.BlockSpec(memory_space=pltpu.SMEM)]
        + [whole(x) for x in (looked, inverse, design)]
        + [pl.BlockSpec(memory_space=pl.ANY)] * len(after),
        out_specs=[whole(x) for x in outputs],
        out_shape=outputs,
        scratch_shapes=[
            pltpu.VMEM((GROUPS * slots, 8 * LANES), jnp.float32),
            pltpu.VMEM((GROUPS * slots, 8, LANES), jnp.float32),
        ],
        compiler_params=pltpu.CompilerParams(vmem_limit_bytes=VMEM_BYTES),
        cost_estimate=lasting(0.02),
        name="invert",
    )(group, looked, inverse, design, *after)


def unpack_kernel(held, out):
    last = DATES - LANES
    out[:, :, :LANES] = held[:, :32]
    packed = held[:, 32:]
    for b in range(4):
        value = packed if b == 0 else pltpu.roll(packed, LANES - b * last, 2)
        out[:, 8 * b : 8 * (b + 1), LANES:] = value[:, :, : last - 1]


def unpack(held):
    output = jax.ShapeDtypeStruct((held.shape[0], 32, DATES - 1), jnp.float32)
    return pl.pallas_call(
        unpack_kernel,
        grid=(1,),
        in_specs=[whole(held)],
        out_specs=whole(output),
        out_shape=output,
        compiler_params=pltpu.CompilerParams(vmem_limit_bytes=8 * 1024 * 1024),
        cost_estimate=lasting(0.3),
        name="unpack",
    )(held)


def tiles(samples):
    ifgs, az, cols = samples.shape
    split = samples.reshape(ifgs, az, cols // LANES, LANES).transpose(0, 2, 1, 3)
    return split.reshape(ifgs * cols // (LANES * RG_LOOKS), PIECES, LANES)


def local(phase_samples, sample_weights, reference_date, secondary_date, window_rows, window_cols):
    ifgs = phase_samples.shape[0]
    row_count = lax.axis_size("rows")
    odd = lax.rem(lax.axis_index("rows"), 2)
    share = (ifgs + 1) // 2
    rest = ifgs - share
    mates = [(r, r ^ 1) for r in range(row_count)]
    outward = [(r, r + 2 if r % 2 else r - 2) for r in range(row_count)]
    outward = [(s, d) for s, d in outward if 0 <= d < row_count]
    across = [(r, r - 2 if r % 2 else r + 2) for r in range(row_count)]
    across = [(s, d) for s, d in across if 0 <= d < row_count]

    group = lax.axis_index("ifg")
    phase = tiles(phase_samples)
    weight = tiles(sample_weights)
    pool = pooling_matrix()
    flip = (1 - 2 * odd).reshape(1)
    side = odd.reshape(1)
    mine = rest * 32 * odd
    other = rest * 32 * (1 - odd)
    slots = 2 * share
    early = FIRST
    late = share - early

    sent_a, looked = look_sums(
        other.reshape(1), early, early // 4, 0, slots, phase, weight, pool
    )
    mate_a = lax.ppermute(sent_a, "rows", mates)
    sent_b, looked = look_sums(
        (other + early * 32).reshape(1), late, late // 3, early, slots, phase, weight, pool, looked
    )
    mate_b = lax.ppermute(sent_b, "rows", mates)
    own_a, looked = look_sums(
        mine.reshape(1), early, early // 4, share, slots, phase, weight, pool, looked
    )
    far_a = lax.ppermute(own_a, "rows", outward)
    own_b, looked = look_sums(
        (mine + early * 32).reshape(1), late, late // 3, share + early, slots,
        phase, weight, pool, looked, (mate_a,),
    )
    far_b = lax.ppermute(own_b, "rows", outward)
    near_a = lax.ppermute(mate_a, "rows", across)
    moved = lax.all_to_all(looked, "ifg", split_axis=0, concat_axis=0, tiled=True)

    dates = jnp.stack([reference_date, secondary_date]).reshape(2, GROUPS, ifgs)
    dates = jnp.where(
        odd == 0,
        jnp.concatenate([dates[:, :, rest:], dates[:, :, :share]], axis=2),
        jnp.concatenate([dates[:, :, :share], dates[:, :, rest:]], axis=2),
    ).reshape(2, -1)
    offsets = (window_rows, window_cols, flip)
    near_b = lax.ppermute(mate_b, "rows", across)
    own_part_a, mate_part_a = window_coherence(
        offsets, near_a, own_a, mate_a, far_a
    )
    back_a = lax.ppermute(mate_part_a, "rows", mates)
    inverse, design = network_solve(flip, dates, slots, (mate_b, mate_part_a))
    *residual, history = invert(
        group.reshape(1), moved, inverse, design, (back_a,)
    )
    residual = residual[:1] + [
        lax.ppermute(residual[d], "ifg", [(i, i ^ d) for i in range(GROUPS)])
        for d in range(1, GROUPS)
    ]
    own_part_b, mate_part_b = window_coherence(
        offsets, near_b, own_b, mate_b, far_b, after=(residual[1], history)
    )
    back_b = lax.ppermute(mate_part_b, "rows", mates)

    residual = unslot(jnp.stack([odd, group]), ifgs, residual, ())
    by_ifg = (-1, 32, LANES)
    coherence = merge(
        side, ifgs, *[part.reshape(by_ifg) for part in (own_part_a, own_part_b, back_a, back_b)],
        after=(residual,),
    )

    history = lax.all_to_all(history, "rows", split_axis=0, concat_axis=0, tiled=True)
    shape = (ifgs, 1, 32 * LANES)
    return (coherence.reshape(shape), residual.reshape(shape), unpack(history).transpose(2, 0, 1))


def solution(mesh):
    placed = (P("ifg", "rows", None), P("ifg", "rows", None), P(), P(), P(), P())
    return jax.shard_map(
        local,
        mesh=mesh,
        in_specs=placed,
        out_specs=(P("ifg", "rows", None), P("ifg", "rows", None), P(None, None, ("ifg", "rows"))),
        check_vma=False,
    )
```
